32 devices in a mesh: dp: 8 (over y, x, core), shard: 4 (over z).
Axes of the slice: x: 2, y: 2, z: 4, core: 2. Of those that a mesh axis runs over, the one named last changes fastest.
Arguments:
- tokens: bfloat16 [16384, 1024], P(('dp', 'shard')), may hold values from -6 to 6
- attn_gain: bfloat16 [1024], P('shard'), may hold values from 0.099609375 to 1.8984375
- w_query: bfloat16 [1024, 2048], P('shard'), may hold values from -0.1875 to 0.1875
- w_key: bfloat16 [1024, 1024], P('shard'), may hold values from -0.1875 to 0.1875
- w_value: bfloat16 [1024, 1024], P('shard'), may hold values from -0.1875 to 0.1875
- q_gain: bfloat16 [128], P('shard'), may hold values from 0.099609375 to 1.8984375
- k_gain: bfloat16 [128], P('shard'), may hold values from 0.099609375 to 1.8984375
- w_out: bfloat16 [2048, 1024], P('shard'), may hold values from -0.75 to 0.75
- mlp_gain: bfloat16 [1024], P('shard'), may hold values from 0.099609375 to 1.8984375
- w_gate: bfloat16 [1024, 3072], P('shard'), may hold values from -0.1875 to 0.1875
- w_up: bfloat16 [1024, 3072], P('shard'), may hold values from -0.1875 to 0.1875
- w_down: bfloat16 [3072, 1024], P('shard'), may hold values from -0.109375 to 0.109375
- segments: int32 [8, 2048], P('dp'), may hold values from 0 to 7, as said below
- spans: int32 [8, 4], P('dp'), may hold values from 0 to 3, each once within a row
- out_grad: bfloat16 [16384, 1024], P(('dp', 'shard')), may hold values from -6 to 6
Outputs:
- result: bfloat16 [16384, 1024], P(('dp', 'shard'))
- grad_tokens: float32 [16384, 1024], P(('dp', 'shard'))
- grad_attn_gain: float32 [1024], P('shard')
- grad_w_query: float32 [1024, 2048], P('shard')
- grad_w_key: float32 [1024, 1024], P('shard')
- grad_w_value: float32 [1024, 1024], P('shard')
- grad_q_gain: float32 [128], P('shard')
- grad_k_gain: float32 [128], P('shard')
- grad_w_out: float32 [2048, 1024], P('shard')
- grad_mlp_gain: float32 [1024], P('shard')
- grad_w_gate: float32 [1024, 3072], P('shard')
- grad_w_up: float32 [1024, 3072], P('shard')
- grad_w_down: float32 [3072, 1024], P('shard')
The draws below stay inside these ranges and needn't reach their ends.
Inputs may be any that keep to these rules, and one draw needn't show every extreme that they name: `segments`: segment numbers never fall along a sequence; positions 0 to 1023 form one document and position 1024 begins another. Each row is a permutation: device j of group i holds sequence blocks spans[i, j] and 7 - spans[i, j].
All inputs are finite; a program needn't handle non-finite values.
Results may differ from the reference program's by a relative error of at most 0.024.
Values may be sent and summed in bfloat16 or wider, within the bound.
No kernel may reach another device: no remote copies, remote signals or barrier semaphores. Data moves between devices by JAX's collectives and lax.ppermute only.
A program may use at most 384 MiB of HBM per device.

```python
import jax
import jax.numpy as jnp
from jax import lax

D = 1024
FF = 3072
HEADS = 16
KV_HEADS = 8
HEAD_WIDTH = 128
TOK_DEV = 512
LEN = 2048
TOKENS = 16384
N_DP = 8
N_SHARD = 4


boundary_count = 6


def draw_segments(key, part):
    key = jax.random.fold_in(key, 17)
    cuts = jax.random.randint(key, (N_DP, boundary_count), LEN // 2 + 1, LEN)
    place = jnp.arange(LEN, dtype=jnp.int32)
    later = (place >= LEN // 2).astype(jnp.int32)
    passed = jnp.sum((place[None, None, :] >= cuts[:, :, None]).astype(jnp.int32), axis=1)
    return (later[None, :] + passed).astype(jnp.int32)


def levels(key, dims, pieces, smallest, largest):
    loudness = 1.0
    for position, shards_of in pieces:
        steps = jax.random.uniform(jax.random.fold_in(jax.random.fold_in(key, 6), position), (shards_of,), jnp.float32, smallest / len(pieces), largest / len(pieces))
        loudness = loudness * jnp.repeat(jnp.exp(steps), dims[position] // shards_of).reshape((-1,) + (1,) * (len(dims) - 1 - position))
    return loudness


def bell_draw(key, dims, deviation, reach, cuts=(), kind=jnp.bfloat16):
    drawn = deviation * jax.random.normal(key, dims, jnp.float32)
    if cuts:
        drawn = drawn * levels(key, dims, cuts, -0.22, 0.18)
    return jnp.clip(drawn, -reach, reach).astype(kind)


def setup_inputs(seed: int = 0) -> dict:
    arg_keys = jax.random.split(jax.random.key(seed), 16)
    return {
        "tokens": bell_draw(arg_keys[0], (TOKENS, D), 1.0, 6.0, ((0, 32),)),
        "attn_gain": jnp.clip(1.0 + 0.18 * jax.random.normal(arg_keys[1], (D,), jnp.float32), 0.099609375, 1.8984375).astype(jnp.bfloat16),
        "w_query": bell_draw(arg_keys[2], (D, HEADS * HEAD_WIDTH), D ** -0.5, 0.1875, ((0, 4),)),
        "w_key": bell_draw(arg_keys[3], (D, KV_HEADS * HEAD_WIDTH), D ** -0.5, 0.1875, ((0, 4),)),
        "w_value": bell_draw(arg_keys[4], (D, KV_HEADS * HEAD_WIDTH), D ** -0.5, 0.1875, ((0, 4),)),
        "q_gain": jnp.clip(1.0 + 0.18 * jax.random.normal(arg_keys[5], (HEAD_WIDTH,), jnp.float32), 0.099609375, 1.8984375).astype(jnp.bfloat16),
        "k_gain": jnp.clip(1.0 + 0.18 * jax.random.normal(arg_keys[6], (HEAD_WIDTH,), jnp.float32), 0.099609375, 1.8984375).astype(jnp.bfloat16),
        "w_out": bell_draw(arg_keys[7], (HEADS * HEAD_WIDTH, D), 64 ** -0.5, 0.75, ((0, 4),)),
        "mlp_gain": jnp.clip(1.0 + 0.18 * jax.random.normal(arg_keys[8], (D,), jnp.float32), 0.099609375, 1.8984375).astype(jnp.bfloat16),
        "w_gate": bell_draw(arg_keys[9], (D, FF), D ** -0.5, 0.1875, ((0, 4),)),
        "w_up": bell_draw(arg_keys[10], (D, FF), D ** -0.5, 0.1875, ((0, 4),)),
        "w_down": bell_draw(arg_keys[11], (FF, D), FF ** -0.5, 0.109375, ((0, 4),)),
        "segments": draw_segments(jax.random.fold_in(arg_keys[15], 71), 0),
        "spans": jax.vmap(lambda own: jax.random.permutation(own, N_SHARD))(jax.random.split(arg_keys[13], N_DP)).reshape((N_DP, N_SHARD)).astype(jnp.int32),
        "out_grad": bell_draw(arg_keys[14], (TOKENS, D), 1.0, 6.0, ((0, 32),)),
    }


MATMUL_ACCURACY = lax.Precision.HIGHEST
EPS = 1e-06
THETA = 1000000.0
NEG = -1e+30

@jax.custom_vjp
def low(v):
    return lax.optimization_barrier(v.astype(jnp.bfloat16)).astype(jnp.float32)

@jax.custom_vjp
def low_back(v):
    return v

def low_keep(v):
    return (low(v), None)

def low_pass(kept, grad):
    return (grad,)

def back_keep(v):
    return (v, None)

def back_low(kept, grad):
    return (low(grad),)
low.defvjp(low_keep, low_pass)
low_back.defvjp(back_keep, back_low)

def matmul(left, right):
    return jnp.dot(left, right, precision=MATMUL_ACCURACY, preferred_element_type=jnp.float32)

def rms_norm(values, gain):
    return values * lax.rsqrt(lax.optimization_barrier(jnp.mean(values * values, axis=-1, keepdims=True)) + EPS) * gain

def rope_tables(positions):
    steps = jnp.arange(HEAD_WIDTH // 2, dtype=jnp.float32) * (2.0 / HEAD_WIDTH)
    inverse = jnp.power(jnp.float32(THETA), -steps)
    angles = positions.astype(jnp.float32)[:, None] * inverse[None, :]
    angles = jnp.concatenate([angles, angles], axis=1)[:, None, :]
    return (jnp.cos(angles), jnp.sin(angles))

def rotate(values, cosine, sine):
    first = values[..., :HEAD_WIDTH // 2]
    second = values[..., HEAD_WIDTH // 2:]
    turned = jnp.concatenate([-second, first], axis=-1)
    return values * cosine + turned * sine

def layout(segment_row, span_row, shards):
    length = segment_row.shape[0]
    block_len = length // (2 * shards)
    mirror = 2 * shards - 1 - span_row
    blocks = jnp.stack([span_row, mirror], axis=1).reshape(2 * shards).astype(jnp.int32)
    offsets = jnp.arange(block_len, dtype=jnp.int32)
    place = (blocks[:, None] * block_len + offsets[None, :]).reshape(length).astype(jnp.int32)
    indices = jnp.arange(length, dtype=jnp.int32)
    fresh = jnp.concatenate([jnp.ones((1,), jnp.bool_), segment_row[1:] != segment_row[:-1]])
    doc_start = lax.cummax(jnp.where(fresh, indices, 0).astype(jnp.int32), axis=0)
    seg_blocks = segment_row.reshape(2 * shards, block_len)
    start_blocks = doc_start.reshape(2 * shards, block_len)
    seg_tok = jnp.take(seg_blocks, blocks, axis=0).reshape(length).astype(jnp.int32)
    rope_pos = (place - jnp.take(start_blocks, blocks, axis=0).reshape(length)).astype(jnp.int32)
    return (place, seg_tok, rope_pos)

def attention(q_rot, k_rot, values, place, seg_tok):
    groups = HEADS // KV_HEADS
    count = LEN // TOK_DEV
    q_blocks = q_rot.reshape(count, TOK_DEV, KV_HEADS, groups, HEAD_WIDTH)
    place_blocks = place.reshape(count, TOK_DEV)
    seg_blocks = seg_tok.reshape(count, TOK_DEV)

    def one_block(items):
        query_portion, place_part, seg_part = items
        local_key_rows = low_back(k_rot)
        local_value_rows = low_back(values)
        score_matrix = jnp.einsum('micf,yif->icmy', query_portion, local_key_rows, precision=MATMUL_ACCURACY) * HEAD_WIDTH ** (-0.5)
        score_matrix = low_back(score_matrix)
        allowed = (seg_part[:, None] == seg_tok[None, :]) & (place[None, :] <= place_part[:, None])
        score_matrix = jnp.where(allowed, score_matrix, NEG)
        peak = lax.optimization_barrier(jnp.max(score_matrix, axis=-1, keepdims=True))
        raised = jnp.where(allowed, jnp.exp(score_matrix - peak), 0.0)
        probability_rows = low(raised / lax.optimization_barrier(jnp.sum(raised, axis=-1, keepdims=True)))
        mixed_heads = jnp.einsum('xjvb,bxu->vxju', probability_rows, local_value_rows, precision=MATMUL_ACCURACY)
        return mixed_heads.reshape(TOK_DEV, HEADS * HEAD_WIDTH)
    return lax.map(jax.checkpoint(one_block), (q_blocks, place_blocks, seg_blocks)).reshape(LEN, HEADS * HEAD_WIDTH)

def forward(rows, params, place, seg_tok, rope_pos):
    attn_gain, w_query, w_key, w_value, q_gain, k_gain, w_out, mlp_gain, w_gate, w_up, w_down = params
    normed = low(rms_norm(rows, attn_gain))
    queries = low_back(matmul(normed, w_query)).reshape(LEN, HEADS, HEAD_WIDTH)
    keys_pre = low_back(matmul(normed, w_key)).reshape(LEN, KV_HEADS, HEAD_WIDTH)
    values = low(low_back(matmul(normed, w_value))).reshape(LEN, KV_HEADS, HEAD_WIDTH)
    cosine, sine = rope_tables(rope_pos)
    q_rot = low(rotate(rms_norm(queries, q_gain), cosine, sine))
    q_rot = q_rot.reshape(LEN, KV_HEADS, HEADS // KV_HEADS, HEAD_WIDTH)
    k_rot = low(rotate(rms_norm(keys_pre, k_gain), cosine, sine))
    attended = low(low_back(attention(q_rot, k_rot, values, place, seg_tok)))
    residual = rows + low_back(matmul(attended, w_out))
    mixed_heads = low(rms_norm(residual, mlp_gain))
    gate = low_back(matmul(mixed_heads, w_gate))
    upward = low_back(matmul(mixed_heads, w_up))
    hidden = low(jax.nn.silu(gate) * upward)
    return residual + low_back(matmul(hidden, w_down))

def reference(tokens, attn_gain, w_query, w_key, w_value, q_gain, k_gain, w_out, mlp_gain, w_gate, w_up, w_down, segments, spans, out_grad):
    weights = (attn_gain.astype(jnp.float32), w_query.astype(jnp.float32), w_key.astype(jnp.float32), w_value.astype(jnp.float32), q_gain.astype(jnp.float32), k_gain.astype(jnp.float32), w_out.astype(jnp.float32), mlp_gain.astype(jnp.float32), w_gate.astype(jnp.float32), w_up.astype(jnp.float32), w_down.astype(jnp.float32))
    inputs = tokens.astype(jnp.float32).reshape(N_DP, LEN, D)
    cotangents = out_grad.astype(jnp.float32).reshape(N_DP, LEN, D)

    def step(totals, item):
        rows, cotangent, segment_row, span_row = item
        place, seg_tok, rope_pos = layout(segment_row, span_row, N_SHARD)

        def apply(values, params):
            return forward(values, params, place, seg_tok, rope_pos)
        outputs, pull = jax.vjp(apply, rows, weights)
        grad_rows, grad_params = pull(cotangent)
        totals = jax.tree.map(lambda left, right: left + right, totals, grad_params)
        return (totals, (outputs.astype(jnp.bfloat16), grad_rows))
    start = jax.tree.map(jnp.zeros_like, weights)
    totals, (outputs, grad_rows) = lax.scan(step, start, (inputs, cotangents, segments, spans))
    return (outputs.reshape(TOKENS, D), grad_rows.reshape(TOKENS, D), totals[0], totals[1], totals[2], totals[3], totals[4], totals[5], totals[6], totals[7], totals[8], totals[9], totals[10])
```

```python
import functools
import math

import jax
import jax.numpy as jnp
from jax import lax
from jax.experimental import pallas as pl
from jax.experimental.pallas import tpu as pltpu
from jax.sharding import PartitionSpec as P

HEADS = 16
KV_HEADS = 8
HEAD_WIDTH = 128
EPS = 1e-06
THETA = 1000000.0
F32 = jnp.float32
BF16 = jnp.bfloat16
SCALE = HEAD_WIDTH ** (-0.5)
EXP2_SCALE = SCALE * math.log2(math.e)
VMEM_LIMIT = 40 * 1024 * 1024


def dp_swap(x, bit):
    count = lax.axis_size("dp")
    return lax.ppermute(x, "dp", [(i, i ^ (1 << bit)) for i in range(count)])


def z_shift(x, step):
    count = lax.axis_size("shard")
    return lax.ppermute(x, "shard", [(i, (i + step) % count) for i in range(count)])


def bit_of(index, bit):
    return (index >> bit) & 1


def plane_order(flip):
    bits = list(range(1, lax.axis_size("dp").bit_length() - 1))
    return bits[::-1] if flip else bits


def column_piece(index, order):
    piece = bit_of(index, 0)
    for bit in order:
        piece = piece * 2 + bit_of(index, bit)
    return piece


def spread(arrays, bits):
    masks = [0]
    for bit in bits:
        arrays = arrays + [dp_swap(a, bit) for a in arrays]
        masks = masks + [m ^ (1 << bit) for m in masks]
    return arrays, masks


def place_kernel(shards, at_ref, own_ref, *refs):
    count = len(refs) - 2
    out_ref, sems = refs[-2], refs[-1]
    rows = own_ref.shape[0]
    cols = refs[0].shape[2]
    copies = [
        pltpu.make_async_copy(
            own_ref, out_ref.at[pl.ds(pl.multiple_of(at_ref[0] * rows, rows), rows), :], sems.at[0]
        )
    ]
    for i in range(count):
        column = pl.multiple_of(at_ref[shards + i] * cols, cols)
        for t in range(1, shards):
            row = pl.multiple_of(at_ref[t] * rows, rows)
            copies.append(
                pltpu.make_async_copy(
                    refs[i].at[t - 1],
                    out_ref.at[pl.ds(row, rows), pl.ds(column, cols)],
                    sems.at[1 + i * (shards - 1) + t - 1],
                )
            )
    for copy in copies:
        copy.start()
    for copy in copies:
        copy.wait()


def gather_weight(own, flip):
    shards = lax.axis_size("shard")
    z = lax.axis_index("shard")
    d = lax.axis_index("dp")
    order = plane_order(flip)
    rows, width = own.shape
    cols = width // lax.axis_size("dp")
    moving = lax.dynamic_slice_in_dim(own, column_piece(d, order) * cols, cols, axis=1)
    chunks = []
    for _ in range(shards - 1):
        moving = z_shift(moving, 1)
        chunks.append(moving)
    arrays, masks = spread([jnp.stack(chunks)], order + [0])
    row_at = [(z - t) % shards for t in range(shards)]
    col_at = [column_piece(d ^ m, order) for m in masks]
    if cols % 128 == 0 and rows % 16 == 0:
        at = jnp.stack(row_at + col_at).astype(jnp.int32)
        return pl.pallas_call(
            functools.partial(place_kernel, shards),
            out_shape=jax.ShapeDtypeStruct((shards * rows, width), own.dtype),
            grid_spec=pltpu.PrefetchScalarGridSpec(
                num_scalar_prefetch=1,
                grid=(1,),
                in_specs=[pl.BlockSpec(memory_space=pl.ANY)] * (1 + len(arrays)),
                out_specs=pl.BlockSpec((shards * rows, width), lambda i, at: (0, 0)),
                scratch_shapes=[pltpu.SemaphoreType.DMA((1 + len(arrays) * (shards - 1),))],
            ),
            compiler_params=pltpu.CompilerParams(vmem_limit_bytes=VMEM_LIMIT),
            name="place",
        )(at, own, *arrays)
    full = jnp.zeros((shards * rows, width), own.dtype)
    full = lax.dynamic_update_slice(full, own, (row_at[0] * rows, 0))
    for array, column in zip(arrays, col_at):
        for t in range(1, shards):
            full = lax.dynamic_update_slice(full, array[t - 1], (row_at[t] * rows, column * cols))
    return full


def widen_kernel(at_ref, *refs):
    out_ref = refs[-1]
    step = pl.program_id(0)
    for i in range(len(refs) - 1):

        @pl.when(step == i)
        def _():
            out_ref[...] = refs[i][...].astype(F32)


def reduce_weight(left, right, flip):
    shards = lax.axis_size("shard")
    z = lax.axis_index("shard")
    d = lax.axis_index("dp")
    order = plane_order(flip)
    width = right.shape[1]
    half = width // 2
    core = bit_of(d, 0)

    def product(columns):
        return lax.dot_general(left, columns, (((0,), (0,)), ((), ())), preferred_element_type=F32)

    theirs = product(lax.dynamic_slice_in_dim(right, (1 - core) * half, half, axis=1)).astype(BF16)
    arrived = dp_swap(theirs, 0)
    mine = product(lax.dynamic_slice_in_dim(right, core * half, half, axis=1))
    total = (mine + arrived.astype(F32)).astype(BF16)
    for bit in order:
        half = half // 2
        here = bit_of(d, bit)
        sent = lax.dynamic_slice_in_dim(total, (1 - here) * half, half, axis=1)
        kept = lax.dynamic_slice_in_dim(total, here * half, half, axis=1)
        total = (kept.astype(F32) + dp_swap(sent, bit).astype(F32)).astype(BF16)
    rows = total.shape[0] // shards

    def chunk(owner):
        return lax.dynamic_slice_in_dim(total, (owner % shards) * rows, rows, axis=0)

    moving = chunk(z - 1 + shards)
    for t in range(1, shards):
        moving = z_shift(moving, 1)
        moving = (moving.astype(F32) + chunk(z - 1 - t + shards).astype(F32)).astype(BF16)
    arrays, masks = spread([moving], order[::-1] + [0])
    col_at = [column_piece(d ^ m, order) for m in masks]
    cols = moving.shape[1]
    if cols % 128 == 0:
        return pl.pallas_call(
            widen_kernel,
            out_shape=jax.ShapeDtypeStruct((rows, width), F32),
            grid_spec=pltpu.PrefetchScalarGridSpec(
                num_scalar_prefetch=1,
                grid=(len(arrays),),
                in_specs=[pl.BlockSpec((rows, cols), lambda i, at: (0, 0))] * len(arrays),
                out_specs=pl.BlockSpec((rows, cols), lambda i, at: (0, at[i])),
            ),
            name="widen",
        )(jnp.stack(col_at).astype(jnp.int32), *arrays)
    full = jnp.zeros((rows, width), F32)
    for array, column in zip(arrays, col_at):
        full = lax.dynamic_update_slice(full, array.astype(F32), (0, column * cols))
    return full


def dot_nt(a, b):
    return lax.dot_general(a, b, (((1,), (1,)), ((), ())), preferred_element_type=F32)


def dot_tn(a, b):
    return lax.dot_general(a, b, (((0,), (0,)), ((), ())), preferred_element_type=F32)


def dot_nn(a, b):
    return lax.dot_general(a, b, (((1,), (0,)), ((), ())), preferred_element_type=F32)


def inverse_rms(v):
    return lax.rsqrt(jnp.mean(v * v, axis=-1, keepdims=True) + EPS)


def turn(u):
    return pltpu.roll(u, HEAD_WIDTH // 2, 1)


def norm_rope(v, gain, cosine, sine):
    u = v * inverse_rms(v) * gain
    return u * cosine + turn(u) * sine


def norm_rope_back(grad, v, gain, cosine, sine):
    r = inverse_rms(v)
    du = grad * cosine + turn(grad * sine)
    scaled = gain * du
    dv = r * scaled - v * (r * r * r) * jnp.mean(scaled * v, axis=-1, keepdims=True)
    return dv, du * v * r


def masked_exp(q, k, key_place, q_place, q_start):
    scores = dot_nt(q, k)
    allowed = (key_place <= q_place) & (key_place >= q_start)
    return jnp.where(allowed, jnp.exp2(scores * EXP2_SCALE), 0.0)


def load_queries(q_ref, gain_ref, cos_ref, sin_ref, held_ref, block):
    gain = gain_ref[...]
    for slot in range(2):
        rows = slice(slot * block, (slot + 1) * block)
        for head in range(2):
            v = q_ref[rows, head * HEAD_WIDTH : (head + 1) * HEAD_WIDTH]
            rotated = norm_rope(v, gain, cos_ref[rows, :], sin_ref[rows, :])
            held_ref[slot, head * block : (head + 1) * block, :] = rotated.astype(BF16)


def attend_kernel(
    sel_ref, q_ref, k_ref, v_ref, cos_ref, sin_ref, qg_ref, kg_ref, kp_ref, qp_ref, qs_ref,
    out_ref, held, acc, total,
):
    block = q_ref.shape[0] // 2
    pairs = k_ref.shape[0] // block
    load_queries(q_ref, qg_ref, cos_ref, sin_ref, held, block)
    for p in range(pairs):
        rows = slice(p * block, (p + 1) * block)
        slot = p if p < 2 else sel_ref[p - 2]
        k = norm_rope(k_ref[rows, :], kg_ref[...], cos_ref[rows, :], sin_ref[rows, :]).astype(BF16)
        e = masked_exp(held[slot], k, kp_ref[:, rows], qp_ref[slot], qs_ref[slot])
        added = dot_nn(e.astype(BF16), v_ref[rows, :])
        summed = jnp.sum(e, axis=-1, keepdims=True)
        if p < 2:
            acc[slot] = added
            total[slot] = summed
        else:
            acc[slot] += added
            total[slot] += summed
    for slot in range(2):
        value = (acc[slot] / total[slot]).astype(out_ref.dtype)
        for head in range(2):
            out_ref[
                slot * block : (slot + 1) * block, head * HEAD_WIDTH : (head + 1) * HEAD_WIDTH
            ] = value[head * block : (head + 1) * block, :]


def attend_back_kernel(
    sel_ref, q_ref, k_ref, v_ref, cos_ref, sin_ref, qg_ref, kg_ref, kp_ref, qp_ref, qs_ref,
    att_ref, gatt_ref, dq_ref, dk_ref, dv_ref, dqg_ref, dkg_ref,
    held, keys, grads, dots, total, raised, dq_acc,
):
    block = q_ref.shape[0] // 2
    pairs = k_ref.shape[0] // block
    load_queries(q_ref, qg_ref, cos_ref, sin_ref, held, block)
    for slot in range(2):
        rows = slice(slot * block, (slot + 1) * block)
        for head in range(2):
            columns = slice(head * HEAD_WIDTH, (head + 1) * HEAD_WIDTH)
            there = slice(head * block, (head + 1) * block)
            g = gatt_ref[rows, columns]
            grads[slot, there, :] = g
            dots[slot, there, :] = jnp.sum(
                g.astype(F32) * att_ref[rows, columns].astype(F32), axis=-1, keepdims=True
            )
    for p in range(pairs):
        rows = slice(p * block, (p + 1) * block)
        slot = p if p < 2 else sel_ref[p - 2]
        k = norm_rope(k_ref[rows, :], kg_ref[...], cos_ref[rows, :], sin_ref[rows, :]).astype(BF16)
        keys[rows, :] = k
        e = masked_exp(held[slot], k, kp_ref[:, rows], qp_ref[slot], qs_ref[slot])
        raised[p] = e
        summed = jnp.sum(e, axis=-1, keepdims=True)
        if p < 2:
            total[slot] = summed
        else:
            total[slot] += summed
    total[...] = 1.0 / total[...]

    @pl.when(pl.program_id(0) == 0)
    def _():
        dqg_ref[...] = jnp.zeros_like(dqg_ref)
        dkg_ref[...] = jnp.zeros_like(dkg_ref)

    for p in range(pairs):
        rows = slice(p * block, (p + 1) * block)
        slot = p if p < 2 else sel_ref[p - 2]
        g = grads[slot]
        shares = raised[p] * total[slot]
        dshares = dot_nt(g, v_ref[rows, :])
        dscores = (shares * (dshares - dots[slot])).astype(BF16)
        dv_ref[rows, :] = dot_tn(shares.astype(BF16), g).astype(dv_ref.dtype)
        added = dot_nn(dscores, keys[rows, :])
        if p < 2:
            dq_acc[slot] = added
        else:
            dq_acc[slot] += added
        dk = dot_tn(dscores, held[slot]) * SCALE
        dv, dgain = norm_rope_back(
            dk, k_ref[rows, :], kg_ref[...], cos_ref[rows, :], sin_ref[rows, :]
        )
        dk_ref[rows, :] = dv.astype(dk_ref.dtype)
        dkg_ref[...] += jnp.sum(dgain, axis=0, keepdims=True)
    for slot in range(2):
        rows = slice(slot * block, (slot + 1) * block)
        for head in range(2):
            columns = slice(head * HEAD_WIDTH, (head + 1) * HEAD_WIDTH)
            dv, dgain = norm_rope_back(
                dq_acc[slot, head * block : (head + 1) * block, :] * SCALE,
                q_ref[rows, columns],
                qg_ref[...],
                cos_ref[rows, :],
                sin_ref[rows, :],
            )
            dq_ref[rows, columns] = dv.astype(dq_ref.dtype)
            dqg_ref[...] += jnp.sum(dgain, axis=0, keepdims=True)


def attention_specs(count, total):
    pair = HEADS // KV_HEADS * HEAD_WIDTH
    fixed2 = lambda h, sel: (0, 0)
    fixed3 = lambda h, sel: (0, 0, 0)
    by_head = lambda h, sel: (0, h)
    q_spec = pl.BlockSpec((count, pair), by_head)
    k_spec = pl.BlockSpec((total, HEAD_WIDTH), by_head)
    inputs = [
        q_spec,
        k_spec,
        k_spec,
        pl.BlockSpec((total, HEAD_WIDTH), fixed2),
        pl.BlockSpec((total, HEAD_WIDTH), fixed2),
        pl.BlockSpec((1, HEAD_WIDTH), fixed2),
        pl.BlockSpec((1, HEAD_WIDTH), fixed2),
        pl.BlockSpec((1, total), fixed2),
        pl.BlockSpec((2, count, 1), fixed3),
        pl.BlockSpec((2, count, 1), fixed3),
    ]
    return q_spec, k_spec, pl.BlockSpec((1, HEAD_WIDTH), fixed2), inputs


def attend(sel, count, total, operands):
    q_spec, _, _, inputs = attention_specs(count, total)
    return pl.pallas_call(
        attend_kernel,
        out_shape=jax.ShapeDtypeStruct((count, HEADS * HEAD_WIDTH), BF16),
        grid_spec=pltpu.PrefetchScalarGridSpec(
            num_scalar_prefetch=1,
            grid=(KV_HEADS,),
            in_specs=inputs,
            out_specs=q_spec,
            scratch_shapes=[
                pltpu.VMEM((2, count, HEAD_WIDTH), BF16),
                pltpu.VMEM((2, count, HEAD_WIDTH), F32),
                pltpu.VMEM((2, count, 1), F32),
            ],
        ),
        compiler_params=pltpu.CompilerParams(vmem_limit_bytes=VMEM_LIMIT),
        name="attend",
    )(sel, *operands)


def attend_back(sel, count, total, operands):
    q_spec, k_spec, gain_spec, inputs = attention_specs(count, total)
    block = count // 2
    width = KV_HEADS * HEAD_WIDTH
    return pl.pallas_call(
        attend_back_kernel,
        out_shape=(
            jax.ShapeDtypeStruct((count, HEADS * HEAD_WIDTH), BF16),
            jax.ShapeDtypeStruct((total, width), BF16),
            jax.ShapeDtypeStruct((total, width), BF16),
            jax.ShapeDtypeStruct((1, HEAD_WIDTH), F32),
            jax.ShapeDtypeStruct((1, HEAD_WIDTH), F32),
        ),
        grid_spec=pltpu.PrefetchScalarGridSpec(
            num_scalar_prefetch=1,
            grid=(KV_HEADS,),
            in_specs=inputs + [q_spec, q_spec],
            out_specs=[q_spec, k_spec, k_spec, gain_spec, gain_spec],
            scratch_shapes=[
                pltpu.VMEM((2, count, HEAD_WIDTH), BF16),
                pltpu.VMEM((total, HEAD_WIDTH), BF16),
                pltpu.VMEM((2, count, HEAD_WIDTH), BF16),
                pltpu.VMEM((2, count, 1), F32),
                pltpu.VMEM((2, count, 1), F32),
                pltpu.VMEM((total // block, count, block), F32),
                pltpu.VMEM((2, count, HEAD_WIDTH), F32),
            ],
        ),
        compiler_params=pltpu.CompilerParams(vmem_limit_bytes=VMEM_LIMIT),
        name="attend_back",
    )(sel, *operands)


def rms_back(grad, v, gain):
    r = inverse_rms(v)
    scaled = grad * gain
    dv = r * scaled - v * (r * r * r) * jnp.mean(scaled * v, axis=-1, keepdims=True)
    return dv, jnp.sum(grad * v * r, axis=0)


def matmul(a, b):
    return jnp.dot(a, b, preferred_element_type=F32)


def body(
    tokens,
    attn_gain,
    w_query,
    w_key,
    w_value,
    q_gain,
    k_gain,
    w_out,
    mlp_gain,
    w_gate,
    w_up,
    w_down,
    segments,
    spans,
    out_grad,
):
    shards = lax.axis_size("shard")
    z = lax.axis_index("shard")
    count = tokens.shape[0]
    block = count // 2
    total = block * (shards + 1)
    span_row = spans[0]
    segment_row = segments[0]

    def span_of(index):
        return lax.dynamic_index_in_dim(span_row, index % shards, keepdims=False)

    span = span_of(z)
    slots = []
    remote = []
    sel = []
    numbers = [span, 2 * shards - 1 - span]
    for k in range(1, shards):
        slot = jnp.where(span < span_of(z + k), 0, 1)
        slots.append(slot)
        remote.append(z_shift(lax.dynamic_slice_in_dim(tokens, slot * block, block, axis=0), k))
        other = span_of(z - k + shards)
        sel.append(jnp.where(other < span, 0, 1))
        numbers.append(jnp.where(other < span, other, 2 * shards - 1 - other))
    sel = jnp.stack(sel).astype(jnp.int32)

    sizes = [attn_gain.shape[0], mlp_gain.shape[0], q_gain.shape[0], k_gain.shape[0]]
    own_gains = jnp.concatenate([attn_gain, mlp_gain, q_gain, k_gain])
    gains = jnp.stack([own_gains] + [z_shift(own_gains, k) for k in range(1, shards)])
    order = (z - jnp.arange(shards)) % shards
    pick = order[:, None] == jnp.arange(shards)[None, :]
    gains = jnp.sum(jnp.where(pick[:, :, None], gains.astype(F32)[None], 0.0), axis=1)
    parts = []
    start = 0
    for size in sizes:
        parts.append(gains[:, start : start + size].reshape(1, shards * size))
        start += size
    attn_g, mlp_g, q_g, k_g = parts

    full_query = gather_weight(w_query, False)
    full_key = gather_weight(w_key, True)
    full_value = gather_weight(w_value, True)
    full_out = gather_weight(w_out, True)
    full_gate = gather_weight(w_gate, False)
    full_up = gather_weight(w_up, True)
    full_down = gather_weight(w_down, False)

    place = jnp.concatenate([n * block + jnp.arange(block, dtype=jnp.int32) for n in numbers])
    seg = jnp.concatenate([lax.dynamic_slice_in_dim(segment_row, n * block, block) for n in numbers])
    doc_start = jnp.sum((segment_row[None, :] < seg[:, None]).astype(jnp.int32), axis=1)
    steps = jnp.arange(HEAD_WIDTH // 2, dtype=F32) * (2.0 / HEAD_WIDTH)
    inverse = jnp.power(F32(THETA), -steps)
    angles = (place - doc_start).astype(F32)[:, None] * inverse[None, :]
    cosine, sine = jnp.cos(angles), jnp.sin(angles)
    cosine = jnp.concatenate([cosine, cosine], axis=1)
    sine = jnp.concatenate([-sine, sine], axis=1)

    def by_slot(v):
        v = v[:count].reshape(2, 1, block, 1)
        return jnp.concatenate([v, v], axis=1).reshape(2, count, 1)

    rows = jnp.concatenate([tokens] + remote, axis=0).astype(F32)
    normed = (rows * inverse_rms(rows) * attn_g).astype(BF16)
    queries = matmul(normed[:count], full_query)
    keys_pre = matmul(normed, full_key)
    values = matmul(normed, full_value).astype(BF16)
    operands = (
        queries, keys_pre, values, cosine, sine, q_g, k_g,
        place[None, :], by_slot(place), by_slot(doc_start),
    )
    attended = attend(sel, count, total, operands)
    residual = tokens.astype(F32) + matmul(attended, full_out)
    mixed = (residual * inverse_rms(residual) * mlp_g).astype(BF16)
    gate = matmul(mixed, full_gate)
    upward = matmul(mixed, full_up)
    sig = jax.nn.sigmoid(gate)
    hidden = (gate * sig * upward).astype(BF16)
    result = (residual + matmul(hidden, full_down)).astype(BF16)

    grad_w_down = reduce_weight(hidden, out_grad, False)
    grad_hidden = dot_nt(out_grad, full_down)
    grad_gate = (grad_hidden * upward * sig * (1.0 + gate * (1.0 - sig))).astype(BF16)
    grad_upward = (grad_hidden * gate * sig).astype(BF16)
    grad_w_gate = reduce_weight(mixed, grad_gate, False)
    grad_w_up = reduce_weight(mixed, grad_upward, True)
    grad_mixed = dot_nt(grad_gate, full_gate) + dot_nt(grad_upward, full_up)
    grad_residual, grad_mlp_gain = rms_back(grad_mixed, residual, mlp_g)
    grad_residual = grad_residual + out_grad.astype(F32)
    grad_branch = grad_residual.astype(BF16)
    grad_attended = dot_nt(grad_branch, full_out).astype(BF16)
    grad_w_out = reduce_weight(attended, grad_branch, True)

    dq, dk, dv, grad_q_gain, grad_k_gain = attend_back(
        sel, count, total, operands + (attended, grad_attended)
    )
    grad_normed_kv = dot_nt(dk, full_key) + dot_nt(dv, full_value)
    grad_normed_own = grad_normed_kv[:count] + dot_nt(dq, full_query)
    back = []
    for k in range(1, shards):
        term = grad_normed_kv[count + (k - 1) * block : count + k * block].astype(BF16)
        back.append(z_shift(term, shards - k).astype(F32))
    grad_w_query = reduce_weight(normed[:count], dq, False)
    grad_w_key = reduce_weight(normed, dk, True)
    grad_w_value = reduce_weight(normed, dv, True)

    partial = jnp.concatenate([grad_normed_own, grad_normed_kv[count:]], axis=0)
    grad_attn_gain = jnp.sum(partial * rows * inverse_rms(rows), axis=0)
    for slot, term in zip(slots, back):
        first = jnp.where(slot == 0, term, 0.0)
        grad_normed_own = grad_normed_own + jnp.concatenate([first, term - first], axis=0)
    grad_tokens = grad_residual + rms_back(grad_normed_own, tokens.astype(F32), attn_g)[0]

    packed = jnp.concatenate(
        [grad_attn_gain, grad_mlp_gain, grad_q_gain[0], grad_k_gain[0]]
    ).reshape(-1, HEAD_WIDTH)
    for bit in range(lax.axis_size("dp").bit_length() - 1):
        packed = packed + dp_swap(packed, bit)
    packed = sum([z_shift(packed, k) for k in range(1, shards)], packed).reshape(-1)
    gain_grads = []
    start = 0
    for size in sizes:
        gain_grads.append(lax.dynamic_slice_in_dim(packed, start + z * size, size))
        start += size * shards

    return (
        result,
        grad_tokens,
        gain_grads[0],
        grad_w_query,
        grad_w_key,
        grad_w_value,
        gain_grads[2],
        gain_grads[3],
        grad_w_out,
        gain_grads[1],
        grad_w_gate,
        grad_w_up,
        grad_w_down,
    )


def solution(mesh):
    rows = P("shard", None)
    both = P(("dp", "shard"), None)
    placed = (
        both, P("shard"), rows, rows, rows, P("shard"), P("shard"), rows, P("shard"), rows, rows, rows,
        P("dp", None), P("dp", None), both,
    )
    return jax.shard_map(
        body,
        mesh=mesh,
        in_specs=placed,
        out_specs=(
            both, both, P("shard"), rows, rows, rows, P("shard"), P("shard"), rows, P("shard"),
            rows, rows, rows,
        ),
        check_vma=False,
    )
```

```python
import functools
import math

import jax
import jax.numpy as jnp
from jax import lax
from jax.experimental import pallas as pl
from jax.experimental.pallas import tpu as pltpu
from jax.sharding import PartitionSpec as P

HEADS = 16
KV_HEADS = 8
HEAD_WIDTH = 128
EPS = 1e-06
THETA = 1000000.0
F32 = jnp.float32
BF16 = jnp.bfloat16
SCALE = HEAD_WIDTH ** (-0.5)
EXP2_SCALE = SCALE * math.log2(math.e)
VMEM_LIMIT = 48 * 1024 * 1024


def dp_swap(x, bit):
    count = lax.axis_size("dp")
    return lax.ppermute(x, "dp", [(i, i ^ (1 << bit)) for i in range(count)])


def z_shift(x, step):
    count = lax.axis_size("shard")
    return lax.ppermute(x, "shard", [(i, (i + step) % count) for i in range(count)])


def bit_of(index, bit):
    return (index >> bit) & 1


def plane_order(flip):
    bits = list(range(1, lax.axis_size("dp").bit_length() - 1))
    return bits[::-1] if flip else bits


def column_piece(index, order):
    piece = bit_of(index, 0)
    for bit in order:
        piece = piece * 2 + bit_of(index, bit)
    return piece


def spread(arrays, bits):
    masks = [0]
    for bit in bits:
        arrays = arrays + [dp_swap(a, bit) for a in arrays]
        masks = masks + [m ^ (1 << bit) for m in masks]
    return arrays, masks


def place_kernel(shards, at_ref, own_ref, *refs):
    count = len(refs) - 2
    out_ref, sems = refs[-2], refs[-1]
    rows = own_ref.shape[0]
    cols = refs[0].shape[2]
    copies = [
        pltpu.make_async_copy(
            own_ref, out_ref.at[pl.ds(pl.multiple_of(at_ref[0] * rows, rows), rows), :], sems.at[0]
        )
    ]
    for i in range(count):
        column = pl.multiple_of(at_ref[shards + i] * cols, cols)
        for t in range(1, shards):
            row = pl.multiple_of(at_ref[t] * rows, rows)
            copies.append(
                pltpu.make_async_copy(
                    refs[i].at[t - 1],
                    out_ref.at[pl.ds(row, rows), pl.ds(column, cols)],
                    sems.at[1 + i * (shards - 1) + t - 1],
                )
            )
    for copy in copies:
        copy.start()
    for copy in copies:
        copy.wait()


def gather_weight(own, flip):
    shards = lax.axis_size("shard")
    z = lax.axis_index("shard")
    d = lax.axis_index("dp")
    order = plane_order(flip)
    rows, width = own.shape
    cols = width // lax.axis_size("dp")
    moving = lax.dynamic_slice_in_dim(own, column_piece(d, order) * cols, cols, axis=1)
    chunks = []
    for _ in range(shards - 1):
        moving = z_shift(moving, 1)
        chunks.append(moving)
    arrays, masks = spread([jnp.stack(chunks)], order + [0])
    row_at = [(z - t) % shards for t in range(shards)]
    col_at = [column_piece(d ^ m, order) for m in masks]
    if cols % 128 == 0 and rows % 16 == 0:
        at = jnp.stack(row_at + col_at).astype(jnp.int32)
        return pl.pallas_call(
            functools.partial(place_kernel, shards),
            out_shape=jax.ShapeDtypeStruct((shards * rows, width), own.dtype),
            grid_spec=pltpu.PrefetchScalarGridSpec(
                num_scalar_prefetch=1,
                grid=(1,),
                in_specs=[pl.BlockSpec(memory_space=pl.ANY)] * (1 + len(arrays)),
                out_specs=pl.BlockSpec((shards * rows, width), lambda i, at: (0, 0)),
                scratch_shapes=[pltpu.SemaphoreType.DMA((1 + len(arrays) * (shards - 1),))],
            ),
            compiler_params=pltpu.CompilerParams(vmem_limit_bytes=VMEM_LIMIT),
            name="place",
        )(at, own, *arrays)
    full = jnp.zeros((shards * rows, width), own.dtype)
    full = lax.dynamic_update_slice(full, own, (row_at[0] * rows, 0))
    for array, column in zip(arrays, col_at):
        for t in range(1, shards):
            full = lax.dynamic_update_slice(full, array[t - 1], (row_at[t] * rows, column * cols))
    return full


def widen_kernel(at_ref, *refs):
    out_ref = refs[-1]
    step = pl.program_id(0)
    for i in range(len(refs) - 1):

        @pl.when(step == i)
        def _():
            out_ref[...] = refs[i][...].astype(F32)


def reduce_weight(left, right, flip):
    shards = lax.axis_size("shard")
    z = lax.axis_index("shard")
    d = lax.axis_index("dp")
    order = plane_order(flip)
    width = right.shape[1]
    half = width // 2
    core = bit_of(d, 0)

    def product(columns):
        return lax.dot_general(left, columns, (((0,), (0,)), ((), ())), preferred_element_type=F32)

    theirs = product(lax.dynamic_slice_in_dim(right, (1 - core) * half, half, axis=1)).astype(BF16)
    arrived = dp_swap(theirs, 0)
    mine = product(lax.dynamic_slice_in_dim(right, core * half, half, axis=1))
    total = (mine + arrived.astype(F32)).astype(BF16)
    for bit in order:
        half = half // 2
        here = bit_of(d, bit)
        sent = lax.dynamic_slice_in_dim(total, (1 - here) * half, half, axis=1)
        kept = lax.dynamic_slice_in_dim(total, here * half, half, axis=1)
        total = (kept.astype(F32) + dp_swap(sent, bit).astype(F32)).astype(BF16)
    rows = total.shape[0] // shards

    def chunk(owner):
        return lax.dynamic_slice_in_dim(total, (owner % shards) * rows, rows, axis=0)

    moving = chunk(z - 1 + shards)
    for t in range(1, shards):
        moving = z_shift(moving, 1)
        moving = (moving.astype(F32) + chunk(z - 1 - t + shards).astype(F32)).astype(BF16)
    arrays, masks = spread([moving], order[::-1] + [0])
    col_at = [column_piece(d ^ m, order) for m in masks]
    cols = moving.shape[1]
    if cols % 128 == 0:
        return pl.pallas_call(
            widen_kernel,
            out_shape=jax.ShapeDtypeStruct((rows, width), F32),
            grid_spec=pltpu.PrefetchScalarGridSpec(
                num_scalar_prefetch=1,
                grid=(len(arrays),),
                in_specs=[pl.BlockSpec((rows, cols), lambda i, at: (0, 0))] * len(arrays),
                out_specs=pl.BlockSpec((rows, cols), lambda i, at: (0, at[i])),
            ),
            name="widen",
        )(jnp.stack(col_at).astype(jnp.int32), *arrays)
    full = jnp.zeros((rows, width), F32)
    for array, column in zip(arrays, col_at):
        full = lax.dynamic_update_slice(full, array.astype(F32), (0, column * cols))
    return full


def after(done, values):
    return lax.optimization_barrier((done, values))[1]


def stream_masks(order):
    masks = [0]
    for bit in order:
        masks = masks + [m ^ (1 << bit) for m in masks]
    return masks


def pieces_of(order, core_last=True):
    d = lax.axis_index("dp")
    masks = stream_masks(order)
    masks = masks + [m ^ 1 for m in masks] if core_last else masks
    return masks, [column_piece(d ^ m, order) for m in masks]


def place_units_kernel(shards, unit, width, units, offset, counts, at_ref, own_ref, *refs):
    out_ref, sems = refs[-2], refs[-1]
    rows = units * unit
    zero = pl.multiple_of(at_ref[0] * rows, rows)
    copies = [pltpu.make_async_copy(own_ref, out_ref.at[pl.ds(zero, rows), :], sems.at[0])]
    piece = 0
    for i, count in enumerate(counts):
        for e in range(count):
            column = pl.multiple_of(at_ref[shards + piece] * width, width)
            for t in range(1, shards):
                for u in range(units):
                    row = pl.multiple_of(at_ref[t] * rows + u * unit, unit)
                    source = refs[i].at[
                        e, t - 1, :, offset + u * width : offset + (u + 1) * width
                    ]
                    copies.append(
                        pltpu.make_async_copy(
                            source,
                            out_ref.at[pl.ds(row, unit), pl.ds(column, width)],
                            sems.at[len(copies)],
                        )
                    )
            piece += 1
    for copy in copies:
        copy.start()
    for copy in copies:
        copy.wait()


def place_units(own, arrays, unit, offset, flip):
    shards = lax.axis_size("shard")
    z = lax.axis_index("shard")
    rows, total = own.shape
    width = total // lax.axis_size("dp")
    units = rows // unit
    _, columns = pieces_of(plane_order(flip))
    at = jnp.stack([(z - t) % shards for t in range(shards)] + columns).astype(jnp.int32)
    counts = [a.shape[0] for a in arrays]
    return pl.pallas_call(
        functools.partial(place_units_kernel, shards, unit, width, units, offset, counts),
        out_shape=jax.ShapeDtypeStruct((shards * rows, total), own.dtype),
        grid_spec=pltpu.PrefetchScalarGridSpec(
            num_scalar_prefetch=1,
            grid=(1,),
            in_specs=[pl.BlockSpec(memory_space=pl.ANY)] * (1 + len(arrays)),
            out_specs=pl.BlockSpec((shards * rows, total), lambda i, at: (0, 0)),
            scratch_shapes=[pltpu.SemaphoreType.DMA((1 + sum(counts) * (shards - 1) * units,))],
        ),
        compiler_params=pltpu.CompilerParams(vmem_limit_bytes=VMEM_LIMIT),
        name="place",
    )(at, own, *arrays)


def own_piece(own, unit, flip):
    order = plane_order(flip)
    rows, total = own.shape
    width = total // lax.axis_size("dp")
    piece = lax.dynamic_slice_in_dim(
        own, column_piece(lax.axis_index("dp"), order) * width, width, axis=1
    )
    return jnp.concatenate(jnp.split(piece, rows // unit, axis=0), axis=1)


def grow(streams, step):
    bits = [plane_order(bool(s))[step] for s in range(len(streams))]
    return [dp_swap(x, bit) for x, bit in zip(streams, bits)]


def join(held, arrived):
    return [jnp.concatenate([a, b], axis=0) for a, b in zip(held, arrived)]


def grads_kernel(units, items, counts, at_ref, *refs):
    lefts, rights, arrived, outs, turned = [], [], [], [], []
    start = 0
    for group, count in zip((lefts, rights, arrived, outs, turned), counts):
        group.extend(refs[start : start + count])
        start += count

    @pl.when(pl.program_id(0) == 0)
    def _():
        for u, (left, starts, size) in enumerate(units):
            for a, first in enumerate(starts):
                turned[u][a * size : (a + 1) * size, :] = lefts[left][:, first : first + size].T

    for stream, unit, right, offset, width in items:
        rows = rights[right].shape[0]
        pair = jnp.concatenate([rights[right][...], rights[right + 1][...]], axis=1)
        value = dot_nn(turned[unit][:, :rows], pair)
        columns = slice(offset, offset + width)
        for i in range(2):
            part = value[:, i * width : (i + 1) * width]
            if arrived:
                part = part + arrived[stream][i, :, columns].astype(F32)
            outs[stream][i, :, columns] = part.astype(BF16)


def grads(streams, unit, own, arrived=()):
    shards = lax.axis_size("shard")
    d = lax.axis_index("dp")
    lefts, units, rights, right_specs, items, widths, at = [], [], [], [], [], [], []
    unit_index = {}
    pieces = lax.axis_size("dp") // 2
    for s, stream in enumerate(streams):
        order = plane_order(bool(s))
        at += [column_piece(d ^ m ^ (0 if own else 1), order) for m in stream_masks(order)]
        offset = 0
        for left, right in stream:
            width = right.shape[1] // (2 * pieces)
            for i in range(2):
                rights.append(right)
                right_specs.append(
                    pl.BlockSpec(
                        (right.shape[0], width),
                        lambda e, at, s=s, i=i: (0, at[s * pieces + 2 * e + i]),
                    )
                )
            rows = left.shape[1] // shards
            for u in range(rows // unit):
                if (id(left), u) not in unit_index:
                    known = [i for i, x in enumerate(lefts) if x is left]
                    if not known:
                        lefts.append(left)
                    index = known[0] if known else len(lefts) - 1
                    unit_index[id(left), u] = len(units)
                    units.append((index, [k * rows + u * unit for k in range(shards)], unit))
                items.append((s, unit_index[id(left), u], len(rights) - 2, offset, width))
                offset += width
        widths.append(offset)
    out_specs = [pl.BlockSpec((2, shards * unit, w), lambda e, at: (e, 0, 0)) for w in widths]
    counts = (len(lefts), len(rights), len(arrived), len(widths), len(units))
    flops = sum(2 * rights[i[2]].shape[0] * shards * unit * i[4] for i in items) * pieces
    return pl.pallas_call(
        functools.partial(grads_kernel, units, items, counts),
        out_shape=[jax.ShapeDtypeStruct((pieces, shards * unit, w), BF16) for w in widths],
        grid_spec=pltpu.PrefetchScalarGridSpec(
            num_scalar_prefetch=1,
            grid=(pieces // 2,),
            in_specs=[pl.BlockSpec(x.shape, lambda e, at: (0, 0)) for x in lefts]
            + right_specs
            + out_specs[: len(arrived)],
            out_specs=out_specs,
            scratch_shapes=[
                pltpu.VMEM((shards * unit, lefts[u[0]].shape[0]), BF16) for u in units
            ],
        ),
        compiler_params=pltpu.CompilerParams(vmem_limit_bytes=VMEM_LIMIT),
        cost_estimate=pl.CostEstimate(
            flops=flops, bytes_accessed=8 * pieces * shards * unit * sum(widths), transcendentals=0
        ),
        name="grads",
    )(jnp.stack(at).astype(jnp.int32), *lefts, *rights, *arrived)


def fold_sent(streams):
    return [x[x.shape[0] // 2 :] for x in streams]


def fold(streams, arrived):
    return [
        (x[: x.shape[0] // 2].astype(F32) + a.astype(F32)).astype(BF16)
        for x, a in zip(streams, arrived)
    ]


def fold_swap(sent, step):
    bits = [plane_order(bool(s))[::-1][step] for s in range(len(sent))]
    return [dp_swap(x, bit) for x, bit in zip(sent, bits)]


def z_parts(streams, unit):
    shards = lax.axis_size("shard")
    z = lax.axis_index("shard")
    whole = jnp.concatenate([x[0] for x in streams], axis=1) if len(streams) > 1 else streams[0][0]

    def part(k):
        return lax.dynamic_slice_in_dim(whole, ((z + k) % shards) * unit, unit, axis=0)

    return part(0), [part(k) for k in range(1, shards)]


def z_sum(mine, arrived, streams):
    total = mine.astype(F32)
    for a in arrived:
        total = total + a.astype(F32)
    total = total.astype(BF16)
    parts, start = [], 0
    for x in streams:
        parts.append(total[None, :, start : start + x.shape[2]])
        start += x.shape[2]
    return parts


def widen_units_kernel(unit, parts, pieces, at_ref, *refs):
    step = pl.program_id(0)
    outs = refs[-len(parts) :]

    def move(far):
        for out_ref, (stream, offset, units, width) in zip(outs, parts):
            ref = refs[2 * stream + far]
            for u in range(units):
                out_ref[u * unit : (u + 1) * unit, :] = ref[
                    0, :, offset + u * width : offset + (u + 1) * width
                ].astype(F32)

    @pl.when(step < pieces)
    def _():
        move(0)

    @pl.when(step >= pieces)
    def _():
        move(1)


def widen_units(bundle, unit, weights):
    count_dp = lax.axis_size("dp")
    columns, specs, operands, parts, out_specs, shapes = [], [], [], [], [], []
    offsets = [0] * len(bundle)
    for s, (near, far) in enumerate(bundle):
        pieces = near.shape[0]
        columns += pieces_of(plane_order(bool(s)))[1]
        taken = (1,) + near.shape[1:]
        specs += [
            pl.BlockSpec(taken, lambda i, at: (jnp.minimum(i, pieces - 1), 0, 0)),
            pl.BlockSpec(taken, lambda i, at: (jnp.maximum(i - pieces, 0), 0, 0)),
        ]
        operands += [near, far]
    for w, s in weights:
        rows, total = w.shape
        width = total // count_dp
        parts.append((s, offsets[s], rows // unit, width))
        offsets[s] += rows // unit * width
        shapes.append(jax.ShapeDtypeStruct((rows, total), F32))
        out_specs.append(
            pl.BlockSpec((rows, width), lambda i, at, s=s: (0, at[s * count_dp + i]))
        )
    return pl.pallas_call(
        functools.partial(widen_units_kernel, unit, parts, pieces),
        out_shape=shapes,
        grid_spec=pltpu.PrefetchScalarGridSpec(
            num_scalar_prefetch=1, grid=(count_dp,), in_specs=specs, out_specs=out_specs
        ),
        compiler_params=pltpu.CompilerParams(vmem_limit_bytes=VMEM_LIMIT),
        name="widen",
    )(jnp.stack(columns).astype(jnp.int32), *operands)


def dot_nt(a, b):
    return lax.dot_general(a, b, (((1,), (1,)), ((), ())), preferred_element_type=F32)


def dot_tn(a, b):
    return lax.dot_general(a, b, (((0,), (0,)), ((), ())), preferred_element_type=F32)


def dot_nn(a, b):
    return lax.dot_general(a, b, (((1,), (0,)), ((), ())), preferred_element_type=F32)


def inverse_rms(v):
    return lax.rsqrt(jnp.mean(v * v, axis=-1, keepdims=True) + EPS)


def turn(u):
    return pltpu.roll(u, HEAD_WIDTH // 2, 1)


def norm_rope(v, gain, cosine, sine):
    u = v * inverse_rms(v) * gain
    return u * cosine + turn(u) * sine


def norm_rope_back(grad, v, gain, cosine, sine):
    r = inverse_rms(v)
    du = grad * cosine + turn(grad * sine)
    scaled = gain * du
    dv = r * scaled - v * (r * r * r) * jnp.mean(scaled * v, axis=-1, keepdims=True)
    return dv, du * v * r


def masked_exp(q, k, key_place, q_place, q_start):
    scores = dot_nt(q, k)
    allowed = (key_place <= q_place) & (key_place >= q_start)
    return jnp.where(allowed, jnp.exp2(scores * EXP2_SCALE), 0.0)


def load_queries(q_ref, gain_ref, cos_ref, sin_ref, held_ref, block):
    gain = gain_ref[...]
    for slot in range(2):
        rows = slice(slot * block, (slot + 1) * block)
        for head in range(2):
            v = q_ref[rows, head * HEAD_WIDTH : (head + 1) * HEAD_WIDTH]
            rotated = norm_rope(v, gain, cos_ref[rows, :], sin_ref[rows, :])
            held_ref[slot, head * block : (head + 1) * block, :] = rotated.astype(BF16)


def attend_kernel(
    sel_ref, q_ref, k_ref, v_ref, cos_ref, sin_ref, qg_ref, kg_ref, kp_ref, qp_ref, qs_ref,
    out_ref, held, acc, total,
):
    block = q_ref.shape[0] // 2
    pairs = k_ref.shape[0] // block
    load_queries(q_ref, qg_ref, cos_ref, sin_ref, held, block)
    for p in range(pairs):
        rows = slice(p * block, (p + 1) * block)
        slot = p if p < 2 else sel_ref[p - 2]
        k = norm_rope(k_ref[rows, :], kg_ref[...], cos_ref[rows, :], sin_ref[rows, :]).astype(BF16)
        e = masked_exp(held[slot], k, kp_ref[:, rows], qp_ref[slot], qs_ref[slot])
        added = dot_nn(e.astype(BF16), v_ref[rows, :])
        summed = jnp.sum(e, axis=-1, keepdims=True)
        if p < 2:
            acc[slot] = added
            total[slot] = summed
        else:
            acc[slot] += added
            total[slot] += summed
    for slot in range(2):
        value = (acc[slot] / total[slot]).astype(out_ref.dtype)
        for head in range(2):
            out_ref[
                slot * block : (slot + 1) * block, head * HEAD_WIDTH : (head + 1) * HEAD_WIDTH
            ] = value[head * block : (head + 1) * block, :]


def attend_back_kernel(
    sel_ref, q_ref, k_ref, v_ref, cos_ref, sin_ref, qg_ref, kg_ref, kp_ref, qp_ref, qs_ref,
    att_ref, gatt_ref, dq_ref, dk_ref, dv_ref, dqg_ref, dkg_ref,
    held, keys, grads, dots, total, raised, dq_acc,
):
    block = q_ref.shape[0] // 2
    pairs = k_ref.shape[0] // block
    load_queries(q_ref, qg_ref, cos_ref, sin_ref, held, block)
    for slot in range(2):
        rows = slice(slot * block, (slot + 1) * block)
        for head in range(2):
            columns = slice(head * HEAD_WIDTH, (head + 1) * HEAD_WIDTH)
            there = slice(head * block, (head + 1) * block)
            g = gatt_ref[rows, columns]
            grads[slot, there, :] = g
            dots[slot, there, :] = jnp.sum(
                g.astype(F32) * att_ref[rows, columns].astype(F32), axis=-1, keepdims=True
            )
    for p in range(pairs):
        rows = slice(p * block, (p + 1) * block)
        slot = p if p < 2 else sel_ref[p - 2]
        k = norm_rope(k_ref[rows, :], kg_ref[...], cos_ref[rows, :], sin_ref[rows, :]).astype(BF16)
        keys[rows, :] = k
        e = masked_exp(held[slot], k, kp_ref[:, rows], qp_ref[slot], qs_ref[slot])
        raised[p] = e
        summed = jnp.sum(e, axis=-1, keepdims=True)
        if p < 2:
            total[slot] = summed
        else:
            total[slot] += summed
    total[...] = 1.0 / total[...]

    @pl.when(pl.program_id(0) == 0)
    def _():
        dqg_ref[...] = jnp.zeros_like(dqg_ref)
        dkg_ref[...] = jnp.zeros_like(dkg_ref)

    for p in range(pairs):
        rows = slice(p * block, (p + 1) * block)
        slot = p if p < 2 else sel_ref[p - 2]
        g = grads[slot]
        shares = raised[p] * total[slot]
        dshares = dot_nt(g, v_ref[rows, :])
        dscores = (shares * (dshares - dots[slot])).astype(BF16)
        dv_ref[rows, :] = dot_tn(shares.astype(BF16), g).astype(dv_ref.dtype)
        added = dot_nn(dscores, keys[rows, :])
        if p < 2:
            dq_acc[slot] = added
        else:
            dq_acc[slot] += added
        dk = dot_tn(dscores, held[slot]) * SCALE
        dv, dgain = norm_rope_back(
            dk, k_ref[rows, :], kg_ref[...], cos_ref[rows, :], sin_ref[rows, :]
        )
        dk_ref[rows, :] = dv.astype(dk_ref.dtype)
        dkg_ref[...] += jnp.sum(dgain, axis=0, keepdims=True)
    for slot in range(2):
        rows = slice(slot * block, (slot + 1) * block)
        for head in range(2):
            columns = slice(head * HEAD_WIDTH, (head + 1) * HEAD_WIDTH)
            dv, dgain = norm_rope_back(
                dq_acc[slot, head * block : (head + 1) * block, :] * SCALE,
                q_ref[rows, columns],
                qg_ref[...],
                cos_ref[rows, :],
                sin_ref[rows, :],
            )
            dq_ref[rows, columns] = dv.astype(dq_ref.dtype)
            dqg_ref[...] += jnp.sum(dgain, axis=0, keepdims=True)


def attention_specs(count, total):
    pair = HEADS // KV_HEADS * HEAD_WIDTH
    fixed2 = lambda h, sel: (0, 0)
    fixed3 = lambda h, sel: (0, 0, 0)
    by_head = lambda h, sel: (0, h)
    q_spec = pl.BlockSpec((count, pair), by_head)
    k_spec = pl.BlockSpec((total, HEAD_WIDTH), by_head)
    inputs = [
        q_spec,
        k_spec,
        k_spec,
        pl.BlockSpec((total, HEAD_WIDTH), fixed2),
        pl.BlockSpec((total, HEAD_WIDTH), fixed2),
        pl.BlockSpec((1, HEAD_WIDTH), fixed2),
        pl.BlockSpec((1, HEAD_WIDTH), fixed2),
        pl.BlockSpec((1, total), fixed2),
        pl.BlockSpec((2, count, 1), fixed3),
        pl.BlockSpec((2, count, 1), fixed3),
    ]
    return q_spec, k_spec, pl.BlockSpec((1, HEAD_WIDTH), fixed2), inputs


def attention_cost(count, total, products):
    scores = HEADS * count // 2 * total
    return pl.CostEstimate(
        flops=products * 2 * HEAD_WIDTH * scores,
        bytes_accessed=16 * HEAD_WIDTH * HEADS * total,
        transcendentals=scores,
    )


def attend(sel, count, total, operands):
    q_spec, _, _, inputs = attention_specs(count, total)
    return pl.pallas_call(
        attend_kernel,
        out_shape=jax.ShapeDtypeStruct((count, HEADS * HEAD_WIDTH), BF16),
        grid_spec=pltpu.PrefetchScalarGridSpec(
            num_scalar_prefetch=1,
            grid=(KV_HEADS,),
            in_specs=inputs,
            out_specs=q_spec,
            scratch_shapes=[
                pltpu.VMEM((2, count, HEAD_WIDTH), BF16),
                pltpu.VMEM((2, count, HEAD_WIDTH), F32),
                pltpu.VMEM((2, count, 1), F32),
            ],
        ),
        compiler_params=pltpu.CompilerParams(vmem_limit_bytes=VMEM_LIMIT),
        cost_estimate=attention_cost(count, total, 2),
        name="attend",
    )(sel, *operands)


def attend_back(sel, count, total, operands):
    q_spec, k_spec, gain_spec, inputs = attention_specs(count, total)
    block = count // 2
    width = KV_HEADS * HEAD_WIDTH
    return pl.pallas_call(
        attend_back_kernel,
        out_shape=(
            jax.ShapeDtypeStruct((count, HEADS * HEAD_WIDTH), BF16),
            jax.ShapeDtypeStruct((total, width), BF16),
            jax.ShapeDtypeStruct((total, width), BF16),
            jax.ShapeDtypeStruct((1, HEAD_WIDTH), F32),
            jax.ShapeDtypeStruct((1, HEAD_WIDTH), F32),
        ),
        grid_spec=pltpu.PrefetchScalarGridSpec(
            num_scalar_prefetch=1,
            grid=(KV_HEADS,),
            in_specs=inputs + [q_spec, q_spec],
            out_specs=[q_spec, k_spec, k_spec, gain_spec, gain_spec],
            scratch_shapes=[
                pltpu.VMEM((2, count, HEAD_WIDTH), BF16),
                pltpu.VMEM((total, HEAD_WIDTH), BF16),
                pltpu.VMEM((2, count, HEAD_WIDTH), BF16),
                pltpu.VMEM((2, count, 1), F32),
                pltpu.VMEM((2, count, 1), F32),
                pltpu.VMEM((total // block, count, block), F32),
                pltpu.VMEM((2, count, HEAD_WIDTH), F32),
            ],
        ),
        compiler_params=pltpu.CompilerParams(vmem_limit_bytes=VMEM_LIMIT),
        cost_estimate=attention_cost(count, total, 5),
        name="attend_back",
    )(sel, *operands)


def rms_back(grad, v, gain):
    r = inverse_rms(v)
    scaled = grad * gain
    dv = r * scaled - v * (r * r * r) * jnp.mean(scaled * v, axis=-1, keepdims=True)
    return dv, jnp.sum(grad * v * r, axis=0)


def matmul(a, b):
    return jnp.dot(a, b, preferred_element_type=F32)


def body(
    tokens,
    attn_gain,
    w_query,
    w_key,
    w_value,
    q_gain,
    k_gain,
    w_out,
    mlp_gain,
    w_gate,
    w_up,
    w_down,
    segments,
    spans,
    out_grad,
):
    shards = lax.axis_size("shard")
    z = lax.axis_index("shard")
    count = tokens.shape[0]
    block = count // 2
    total = block * (shards + 1)
    span_row = spans[0]
    segment_row = segments[0]

    def span_of(index):
        return lax.dynamic_index_in_dim(span_row, index % shards, keepdims=False)

    span = span_of(z)
    slots = []
    remote_own = []
    sel = []
    numbers = [span, 2 * shards - 1 - span]
    for k in range(1, shards):
        slot = jnp.where(span < span_of(z + k), 0, 1)
        slots.append(slot)
        remote_own.append(lax.dynamic_slice_in_dim(tokens, slot * block, block, axis=0))
        other = span_of(z - k + shards)
        sel.append(jnp.where(other < span, 0, 1))
        numbers.append(jnp.where(other < span, other, 2 * shards - 1 - other))
    sel = jnp.stack(sel).astype(jnp.int32)

    sizes = [attn_gain.shape[0], mlp_gain.shape[0], q_gain.shape[0], k_gain.shape[0]]
    own_gains = jnp.concatenate([attn_gain, mlp_gain, q_gain, k_gain])
    unit = w_query.shape[0]
    count_dp = lax.axis_size("dp")
    bundled = all(
        w.shape[1] % (128 * count_dp) == 0 and w.shape[0] % unit == 0
        for w in (w_query, w_key, w_value, w_out, w_gate, w_up, w_down)
    ) and count_dp == 8
    if bundled:

        def own_pieces(streams):
            own = [
                jnp.concatenate([own_piece(w, unit, bool(s)) for w in stream], axis=1)
                for s, stream in enumerate(streams)
            ]
            return jnp.concatenate(own, axis=1), own[0].shape[1]

        def fetch(both):
            return [z_shift(both, k) for k in range(1, shards)]

        def streams_of(got, split):
            return [
                jnp.stack([g[:unit, :split] for g in got])[None],
                jnp.stack([g[:unit, split:] for g in got])[None],
            ]

        def widely(held):
            for step in range(1, len(plane_order(False))):
                held = join(held, grow(held, step - 1))
            return held, grow(held, len(plane_order(False)) - 1)

        def cores(held, arrived):
            return [[h, a, dp_swap(h, 0), dp_swap(a, 0)] for h, a in zip(held, arrived)]

        both, split_attn = own_pieces([[w_query], [w_key, w_value]])
        room = 16 * both.shape[1]
        packed = jnp.pad(own_gains, (0, room - own_gains.shape[0])).reshape(16, both.shape[1])
        first = fetch(jnp.concatenate([both, packed], axis=0))
        gains = jnp.stack(
            [own_gains] + [g[unit:].reshape(-1)[: own_gains.shape[0]] for g in first]
        )
        remote = [z_shift(x, k + 1) for k, x in enumerate(after(first, remote_own))]
        held, arrived = widely(streams_of(first, split_attn))
        held, arrived = after(remote, (held, arrived))
        near_q, near_kv = cores(held, arrived)
        both, split_out = own_pieces([[w_gate], [w_out]])
        second = fetch(after((near_q, near_kv), both))
        piece = w_key.shape[1] // count_dp
        full_query = place_units(w_query, near_q, unit, 0, False)
        full_key = place_units(w_key, near_kv, unit, 0, True)
        full_value = place_units(w_value, near_kv, unit, piece, True)
    else:
        gains = jnp.stack([own_gains] + [z_shift(own_gains, k) for k in range(1, shards)])
        remote = [z_shift(x, k + 1) for k, x in enumerate(remote_own)]
        full_query = gather_weight(w_query, False)
        full_key = gather_weight(w_key, True)
        full_value = gather_weight(w_value, True)
        full_out = gather_weight(w_out, True)
        full_gate = gather_weight(w_gate, False)
        full_up = gather_weight(w_up, True)
        full_down = gather_weight(w_down, False)

    order = (z - jnp.arange(shards)) % shards
    pick = order[:, None] == jnp.arange(shards)[None, :]
    gains = jnp.sum(jnp.where(pick[:, :, None], gains.astype(F32)[None], 0.0), axis=1)
    parts = []
    start = 0
    for size in sizes:
        parts.append(gains[:, start : start + size].reshape(1, shards * size))
        start += size
    attn_g, mlp_g, q_g, k_g = parts

    place = jnp.concatenate([n * block + jnp.arange(block, dtype=jnp.int32) for n in numbers])
    seg = jnp.concatenate([lax.dynamic_slice_in_dim(segment_row, n * block, block) for n in numbers])
    doc_start = jnp.sum((segment_row[None, :] < seg[:, None]).astype(jnp.int32), axis=1)
    steps = jnp.arange(HEAD_WIDTH // 2, dtype=F32) * (2.0 / HEAD_WIDTH)
    inverse = jnp.power(F32(THETA), -steps)
    angles = (place - doc_start).astype(F32)[:, None] * inverse[None, :]
    cosine, sine = jnp.cos(angles), jnp.sin(angles)
    cosine = jnp.concatenate([cosine, cosine], axis=1)
    sine = jnp.concatenate([-sine, sine], axis=1)

    def by_slot(v):
        v = v[:count].reshape(2, 1, block, 1)
        return jnp.concatenate([v, v], axis=1).reshape(2, count, 1)

    rows = jnp.concatenate([tokens] + remote, axis=0).astype(F32)
    normed = (rows * inverse_rms(rows) * attn_g).astype(BF16)
    queries = matmul(normed[:count], full_query)
    keys_pre = matmul(normed, full_key)
    values = matmul(normed, full_value).astype(BF16)
    operands = (
        queries, keys_pre, values, cosine, sine, q_g, k_g,
        place[None, :], by_slot(place), by_slot(doc_start),
    )
    if bundled:
        second, operands = lax.optimization_barrier((second, operands))
        both, split_down = own_pieces([[w_up], [w_down]])
        third = fetch(after(second, both))
        held = streams_of(second, split_out)
        held = join(held, grow(held, 0)) if len(plane_order(False)) > 1 else held
    attended = attend(sel, count, total, operands)
    if bundled:
        held, third, attended = lax.optimization_barrier((held, third, attended))
        later = streams_of(third, split_down)
        later_arrived = grow(later, 0)
        arrived = grow(held, 1)
        later, later_arrived, held, arrived = lax.optimization_barrier(
            (later, later_arrived, held, arrived)
        )
        near_gate, near_out = cores(held, arrived)
        later = join(later, later_arrived)
        later, near_gate, near_out = lax.optimization_barrier((later, near_gate, near_out))
        later_arrived = grow(later, 1)
        full_out = place_units(w_out, near_out, unit, 0, True)
        full_gate = place_units(w_gate, near_gate, unit, 0, False)
    residual = tokens.astype(F32) + matmul(attended, full_out)
    mixed = (residual * inverse_rms(residual) * mlp_g).astype(BF16)
    gate = matmul(mixed, full_gate)
    if bundled:
        later_arrived, gate = lax.optimization_barrier((later_arrived, gate))
        near_up, near_down = cores(later, later_arrived)
        full_up = place_units(w_up, near_up, unit, 0, False)
        full_down = place_units(w_down, near_down, unit, 0, True)
    upward = matmul(mixed, full_up)
    sig = jax.nn.sigmoid(gate)
    hidden = (gate * sig * upward).astype(BF16)
    result = (residual + matmul(hidden, full_down)).astype(BF16)

    def swap_cores(streams):
        return [dp_swap(x, 0) for x in streams]

    def z_send(streams, chained=False):
        mine, sent = z_parts(streams, unit)
        got = []
        for k, x in enumerate(sent):
            got.append(z_shift(after(got[-1], x) if chained and got else x, k + 1))
        return mine, got

    barrier = lax.optimization_barrier

    grad_rows = out_grad
    if bundled:
        down_pairs = [[(hidden, out_grad)]]
        theirs = grads(down_pairs, unit, False)
        theirs, grad_rows = barrier((theirs, out_grad))
        down_core = swap_cores(theirs)
    else:
        grad_w_down = reduce_weight(hidden, out_grad, False)
    grad_hidden = dot_nt(grad_rows, full_down)
    grad_gate = (grad_hidden * upward * sig * (1.0 + gate * (1.0 - sig))).astype(BF16)
    grad_upward = (grad_hidden * gate * sig).astype(BF16)
    if bundled:
        down_core, grad_gate, grad_upward = barrier((down_core, grad_gate, grad_upward))
        down_sum = grads(down_pairs, unit, True, down_core)
        down_sum, grad_gate, grad_upward = barrier((down_sum, grad_gate, grad_upward))
        down_first = fold_swap(fold_sent(down_sum), 0)
    grad_mixed = dot_nt(grad_gate, full_gate) + dot_nt(grad_upward, full_up)
    grad_residual, grad_mlp_gain = rms_back(grad_mixed, residual, mlp_g)
    grad_residual = grad_residual + out_grad.astype(F32)
    grad_branch = grad_residual.astype(BF16)
    if bundled:
        mlp_pairs = [[(mixed, grad_gate)], [(mixed, grad_upward), (attended, grad_branch)]]
        theirs = grads(mlp_pairs, unit, False)
        theirs, down_first, branch = barrier((theirs, down_first, grad_branch))
        mlp_core = swap_cores(theirs)
        down_sum = fold(down_sum, down_first)
        down_second = fold_swap(fold_sent(down_sum), 1)
        grad_attended = dot_nt(branch, full_out).astype(BF16)
        mlp_core, down_second, grad_attended = barrier((mlp_core, down_second, grad_attended))
        down_sum = fold(down_sum, down_second)
        down_mine, down_z = z_send(down_sum)
        mlp_sum = grads(mlp_pairs, unit, True, mlp_core)
        mlp_sum, grad_attended = barrier((mlp_sum, grad_attended))
        mlp_first = fold_swap(fold_sent(mlp_sum), 0)
    else:
        grad_attended = dot_nt(grad_branch, full_out).astype(BF16)
        grad_w_gate = reduce_weight(mixed, grad_gate, False)
        grad_w_up = reduce_weight(mixed, grad_upward, True)
        grad_w_out = reduce_weight(attended, grad_branch, True)

    dq, dk, dv, grad_q_gain, grad_k_gain = attend_back(
        sel, count, total, operands + (attended, grad_attended)
    )
    if bundled:
        mlp_first, down_z, dq, dk, dv = barrier((mlp_first, down_z, dq, dk, dv))
        mlp_sum = fold(mlp_sum, mlp_first)
        mlp_second = fold_swap(fold_sent(mlp_sum), 1)
        attn_pairs = [[(normed, dq)], [(normed, dk), (normed, dv)]]
        theirs = grads(attn_pairs, unit, False)
    grad_normed_kv = dot_nt(dk, full_key) + dot_nt(dv, full_value)
    terms = [
        grad_normed_kv[count + (k - 1) * block : count + k * block].astype(BF16)
        for k in range(1, shards)
    ]
    if bundled:
        mlp_second, theirs = barrier((mlp_second, theirs))
        down_sum = z_sum(down_mine, down_z, down_sum)
        attn_core = swap_cores(theirs)
        mlp_sum = fold(mlp_sum, mlp_second)
    back = []
    for k, term in enumerate(terms):
        back.append(z_shift(after(back[-1], term) if back else term, shards - k - 1))
    grad_normed_own = grad_normed_kv[:count] + dot_nt(dq, full_query)
    partial = jnp.concatenate([grad_normed_own, grad_normed_kv[count:]], axis=0)
    grad_attn_gain = jnp.sum(partial * rows * inverse_rms(rows), axis=0)
    gain_sum = jnp.concatenate(
        [grad_attn_gain, grad_mlp_gain, grad_q_gain[0], grad_k_gain[0]]
    ).reshape(-1, HEAD_WIDTH)
    if bundled:
        mlp_mine, mlp_z = z_send(mlp_sum, True)
        attn_core, grad_normed_own = barrier((attn_core, grad_normed_own))
        attn_sum = grads(attn_pairs, unit, True, attn_core)
        attn_first = fold_swap(fold_sent(attn_sum), 0)
        gain_other = dp_swap(gain_sum, 0)
        attn_first, back, gain_other = barrier((attn_first, back, gain_other))
        gain_sum = gain_sum + gain_other
        attn_sum = fold(attn_sum, attn_first)
        attn_second = fold_swap(fold_sent(attn_sum), 1)
        gain_other = dp_swap(gain_sum, 1)
        attn_second, mlp_z, gain_other = barrier((attn_second, mlp_z, gain_other))
        gain_sum = gain_sum + gain_other
        attn_sum = fold(attn_sum, attn_second)
        attn_mine, attn_z = z_send(attn_sum)
        gain_sum = gain_sum + dp_swap(gain_sum, 2)
        mlp_sum = z_sum(mlp_mine, mlp_z, mlp_sum)

        def whole(streams):
            for step in range(len(plane_order(False))):
                streams = join(streams, grow(streams, step))
            return [(x, dp_swap(x, 0)) for x in streams]

        mlp_sum = [jnp.concatenate([down_sum[0], mlp_sum[0]], axis=2), mlp_sum[1]]
        grad_w_down, grad_w_gate, grad_w_up, grad_w_out = widen_units(
            whole(mlp_sum), unit, [(w_down, 0), (w_gate, 0), (w_up, 1), (w_out, 1)]
        )
        attn_z, gain_sum = after(
            (grad_w_down, grad_w_gate, grad_w_up, grad_w_out, gain_sum), (attn_z, gain_sum)
        )
        gain_sum = sum([z_shift(gain_sum, k) for k in range(1, shards)], gain_sum)
        attn_sum = z_sum(attn_mine, attn_z, attn_sum)
        grad_w_query, grad_w_key, grad_w_value = widen_units(
            whole(attn_sum), unit, [(w_query, 0), (w_key, 1), (w_value, 1)]
        )
    else:
        for bit in range(count_dp.bit_length() - 1):
            gain_sum = gain_sum + dp_swap(gain_sum, bit)
        gain_sum = sum([z_shift(gain_sum, k) for k in range(1, shards)], gain_sum)
        grad_w_query = reduce_weight(normed[:count], dq, False)
        grad_w_key = reduce_weight(normed, dk, True)
        grad_w_value = reduce_weight(normed, dv, True)

    for slot, term in zip(slots, back):
        term = term.astype(F32)
        first = jnp.where(slot == 0, term, 0.0)
        grad_normed_own = grad_normed_own + jnp.concatenate([first, term - first], axis=0)
    grad_tokens = grad_residual + rms_back(grad_normed_own, tokens.astype(F32), attn_g)[0]

    packed = gain_sum.reshape(-1)
    gain_grads = []
    start = 0
    for size in sizes:
        gain_grads.append(lax.dynamic_slice_in_dim(packed, start + z * size, size))
        start += size * shards

    return (
        result,
        grad_tokens,
        gain_grads[0],
        grad_w_query,
        grad_w_key,
        grad_w_value,
        gain_grads[2],
        gain_grads[3],
        grad_w_out,
        gain_grads[1],
        grad_w_gate,
        grad_w_up,
        grad_w_down,
    )


def solution(mesh):
    rows = P("shard", None)
    both = P(("dp", "shard"), None)
    placed = (
        both, P("shard"), rows, rows, rows, P("shard"), P("shard"), rows, P("shard"), rows, rows, rows,
        P("dp", None), P("dp", None), both,
    )
    return jax.shard_map(
        body,
        mesh=mesh,
        in_specs=placed,
        out_specs=(
            both, both, P("shard"), rows, rows, rows, P("shard"), P("shard"), rows, P("shard"),
            rows, rows, rows,
        ),
        check_vma=False,
    )
```

```python
import functools
import math

import jax
import jax.numpy as jnp
from jax import lax
from jax.experimental import pallas as pl
from jax.experimental.pallas import tpu as pltpu
from jax.sharding import PartitionSpec as P

HEADS = 16
KV_HEADS = 8
HEAD_WIDTH = 128
EPS = 1e-06
THETA = 1000000.0
F32 = jnp.float32
BF16 = jnp.bfloat16
SCALE = HEAD_WIDTH ** (-0.5)
EXP2_SCALE = SCALE * math.log2(math.e)
VMEM_LIMIT = 48 * 1024 * 1024


def dp_swap(x, bit):
    count = lax.axis_size("dp")
    return lax.ppermute(x, "dp", [(i, i ^ (1 << bit)) for i in range(count)])


def z_shift(x, step):
    count = lax.axis_size("shard")
    return lax.ppermute(x, "shard", [(i, (i + step) % count) for i in range(count)])


def bit_of(index, bit):
    return (index >> bit) & 1


def plane_order(flip):
    bits = list(range(1, lax.axis_size("dp").bit_length() - 1))
    return bits[::-1] if flip else bits


def column_piece(index, order):
    piece = bit_of(index, 0)
    for bit in order:
        piece = piece * 2 + bit_of(index, bit)
    return piece


def spread(arrays, bits):
    masks = [0]
    for bit in bits:
        arrays = arrays + [dp_swap(a, bit) for a in arrays]
        masks = masks + [m ^ (1 << bit) for m in masks]
    return arrays, masks


def place_kernel(shards, at_ref, own_ref, *refs):
    count = len(refs) - 2
    out_ref, sems = refs[-2], refs[-1]
    rows = own_ref.shape[0]
    cols = refs[0].shape[2]
    copies = [
        pltpu.make_async_copy(
            own_ref, out_ref.at[pl.ds(pl.multiple_of(at_ref[0] * rows, rows), rows), :], sems.at[0]
        )
    ]
    for i in range(count):
        column = pl.multiple_of(at_ref[shards + i] * cols, cols)
        for t in range(1, shards):
            row = pl.multiple_of(at_ref[t] * rows, rows)
            copies.append(
                pltpu.make_async_copy(
                    refs[i].at[t - 1],
                    out_ref.at[pl.ds(row, rows), pl.ds(column, cols)],
                    sems.at[1 + i * (shards - 1) + t - 1],
                )
            )
    for copy in copies:
        copy.start()
    for copy in copies:
        copy.wait()


def gather_weight(own, flip):
    shards = lax.axis_size("shard")
    z = lax.axis_index("shard")
    d = lax.axis_index("dp")
    order = plane_order(flip)
    rows, width = own.shape
    cols = width // lax.axis_size("dp")
    moving = lax.dynamic_slice_in_dim(own, column_piece(d, order) * cols, cols, axis=1)
    chunks = []
    for _ in range(shards - 1):
        moving = z_shift(moving, 1)
        chunks.append(moving)
    arrays, masks = spread([jnp.stack(chunks)], order + [0])
    row_at = [(z - t) % shards for t in range(shards)]
    col_at = [column_piece(d ^ m, order) for m in masks]
    if cols % 128 == 0 and rows % 16 == 0:
        at = jnp.stack(row_at + col_at).astype(jnp.int32)
        return pl.pallas_call(
            functools.partial(place_kernel, shards),
            out_shape=jax.ShapeDtypeStruct((shards * rows, width), own.dtype),
            grid_spec=pltpu.PrefetchScalarGridSpec(
                num_scalar_prefetch=1,
                grid=(1,),
                in_specs=[pl.BlockSpec(memory_space=pl.ANY)] * (1 + len(arrays)),
                out_specs=pl.BlockSpec((shards * rows, width), lambda i, at: (0, 0)),
                scratch_shapes=[pltpu.SemaphoreType.DMA((1 + len(arrays) * (shards - 1),))],
            ),
            compiler_params=pltpu.CompilerParams(vmem_limit_bytes=VMEM_LIMIT),
            name="place",
        )(at, own, *arrays)
    full = jnp.zeros((shards * rows, width), own.dtype)
    full = lax.dynamic_update_slice(full, own, (row_at[0] * rows, 0))
    for array, column in zip(arrays, col_at):
        for t in range(1, shards):
            full = lax.dynamic_update_slice(full, array[t - 1], (row_at[t] * rows, column * cols))
    return full


def widen_kernel(at_ref, *refs):
    out_ref = refs[-1]
    step = pl.program_id(0)
    for i in range(len(refs) - 1):

        @pl.when(step == i)
        def _():
            out_ref[...] = refs[i][...].astype(F32)


def reduce_weight(left, right, flip):
    shards = lax.axis_size("shard")
    z = lax.axis_index("shard")
    d = lax.axis_index("dp")
    order = plane_order(flip)
    width = right.shape[1]
    half = width // 2
    core = bit_of(d, 0)

    def product(columns):
        return lax.dot_general(left, columns, (((0,), (0,)), ((), ())), preferred_element_type=F32)

    theirs = product(lax.dynamic_slice_in_dim(right, (1 - core) * half, half, axis=1)).astype(BF16)
    arrived = dp_swap(theirs, 0)
    mine = product(lax.dynamic_slice_in_dim(right, core * half, half, axis=1))
    total = (mine + arrived.astype(F32)).astype(BF16)
    for bit in order:
        half = half // 2
        here = bit_of(d, bit)
        sent = lax.dynamic_slice_in_dim(total, (1 - here) * half, half, axis=1)
        kept = lax.dynamic_slice_in_dim(total, here * half, half, axis=1)
        total = (kept.astype(F32) + dp_swap(sent, bit).astype(F32)).astype(BF16)
    rows = total.shape[0] // shards

    def chunk(owner):
        return lax.dynamic_slice_in_dim(total, (owner % shards) * rows, rows, axis=0)

    moving = chunk(z - 1 + shards)
    for t in range(1, shards):
        moving = z_shift(moving, 1)
        moving = (moving.astype(F32) + chunk(z - 1 - t + shards).astype(F32)).astype(BF16)
    arrays, masks = spread([moving], order[::-1] + [0])
    col_at = [column_piece(d ^ m, order) for m in masks]
    cols = moving.shape[1]
    if cols % 128 == 0:
        return pl.pallas_call(
            widen_kernel,
            out_shape=jax.ShapeDtypeStruct((rows, width), F32),
            grid_spec=pltpu.PrefetchScalarGridSpec(
                num_scalar_prefetch=1,
                grid=(len(arrays),),
                in_specs=[pl.BlockSpec((rows, cols), lambda i, at: (0, 0))] * len(arrays),
                out_specs=pl.BlockSpec((rows, cols), lambda i, at: (0, at[i])),
            ),
            name="widen",
        )(jnp.stack(col_at).astype(jnp.int32), *arrays)
    full = jnp.zeros((rows, width), F32)
    for array, column in zip(arrays, col_at):
        full = lax.dynamic_update_slice(full, array.astype(F32), (0, column * cols))
    return full


def after(done, values):
    return lax.optimization_barrier((done, values))[1]


def stream_masks(order):
    masks = [0]
    for bit in order:
        masks = masks + [m ^ (1 << bit) for m in masks]
    return masks


def pieces_of(order, core_last=True):
    d = lax.axis_index("dp")
    masks = stream_masks(order)
    masks = masks + [m ^ 1 for m in masks] if core_last else masks
    return masks, [column_piece(d ^ m, order) for m in masks]


def place_units_kernel(shards, unit, width, units, offset, counts, at_ref, own_ref, *refs):
    out_ref, sems = refs[-2], refs[-1]
    rows = units * unit
    zero = pl.multiple_of(at_ref[0] * rows, rows)
    copies = [pltpu.make_async_copy(own_ref, out_ref.at[pl.ds(zero, rows), :], sems.at[0])]
    piece = 0
    for i, count in enumerate(counts):
        for e in range(count):
            column = pl.multiple_of(at_ref[shards + piece] * width, width)
            for t in range(1, shards):
                for u in range(units):
                    row = pl.multiple_of(at_ref[t] * rows + u * unit, unit)
                    source = refs[i].at[
                        e, t - 1, :, offset + u * width : offset + (u + 1) * width
                    ]
                    copies.append(
                        pltpu.make_async_copy(
                            source,
                            out_ref.at[pl.ds(row, unit), pl.ds(column, width)],
                            sems.at[len(copies)],
                        )
                    )
            piece += 1
    for copy in copies:
        copy.start()
    for copy in copies:
        copy.wait()


def place_units(own, arrays, unit, offset, flip):
    shards = lax.axis_size("shard")
    z = lax.axis_index("shard")
    rows, total = own.shape
    width = total // lax.axis_size("dp")
    units = rows // unit
    _, columns = pieces_of(plane_order(flip))
    at = jnp.stack([(z - t) % shards for t in range(shards)] + columns).astype(jnp.int32)
    counts = [a.shape[0] for a in arrays]
    return pl.pallas_call(
        functools.partial(place_units_kernel, shards, unit, width, units, offset, counts),
        out_shape=jax.ShapeDtypeStruct((shards * rows, total), own.dtype),
        grid_spec=pltpu.PrefetchScalarGridSpec(
            num_scalar_prefetch=1,
            grid=(1,),
            in_specs=[pl.BlockSpec(memory_space=pl.ANY)] * (1 + len(arrays)),
            out_specs=pl.BlockSpec((shards * rows, total), lambda i, at: (0, 0)),
            scratch_shapes=[pltpu.SemaphoreType.DMA((1 + sum(counts) * (shards - 1) * units,))],
        ),
        compiler_params=pltpu.CompilerParams(vmem_limit_bytes=VMEM_LIMIT),
        name="place",
    )(at, own, *arrays)


def own_piece(own, unit, flip):
    order = plane_order(flip)
    rows, total = own.shape
    width = total // lax.axis_size("dp")
    piece = lax.dynamic_slice_in_dim(
        own, column_piece(lax.axis_index("dp"), order) * width, width, axis=1
    )
    return jnp.concatenate(jnp.split(piece, rows // unit, axis=0), axis=1)


def grow(streams, step):
    bits = [plane_order(bool(s))[step] for s in range(len(streams))]
    return [dp_swap(x, bit) for x, bit in zip(streams, bits)]


def join(held, arrived):
    return [jnp.concatenate([a, b], axis=0) for a, b in zip(held, arrived)]


def grads_kernel(units, items, counts, at_ref, *refs):
    lefts, rights, arrived, outs, turned = [], [], [], [], []
    start = 0
    for group, count in zip((lefts, rights, arrived, outs, turned), counts):
        group.extend(refs[start : start + count])
        start += count

    @pl.when(pl.program_id(0) == 0)
    def _():
        for u, (left, starts, size) in enumerate(units):
            for a, first in enumerate(starts):
                turned[u][a * size : (a + 1) * size, :] = lefts[left][:, first : first + size].T

    for stream, unit, right, offset, width in items:
        rows = rights[right].shape[0]
        pair = jnp.concatenate([rights[right][...], rights[right + 1][...]], axis=1)
        value = dot_nn(turned[unit][:, :rows], pair)
        columns = slice(offset, offset + width)
        for i in range(2):
            part = value[:, i * width : (i + 1) * width]
            if arrived:
                part = part + arrived[stream][i, :, columns].astype(F32)
            outs[stream][i, :, columns] = part.astype(BF16)


def grads(streams, unit, own, arrived=()):
    shards = lax.axis_size("shard")
    d = lax.axis_index("dp")
    lefts, units, rights, right_specs, items, widths, at = [], [], [], [], [], [], []
    unit_index = {}
    pieces = lax.axis_size("dp") // 2
    for s, stream in enumerate(streams):
        order = plane_order(bool(s))
        at += [column_piece(d ^ m ^ (0 if own else 1), order) for m in stream_masks(order)]
        offset = 0
        for left, right in stream:
            width = right.shape[1] // (2 * pieces)
            for i in range(2):
                rights.append(right)
                right_specs.append(
                    pl.BlockSpec(
                        (right.shape[0], width),
                        lambda e, at, s=s, i=i: (0, at[s * pieces + 2 * e + i]),
                    )
                )
            rows = left.shape[1] // shards
            for u in range(rows // unit):
                if (id(left), u) not in unit_index:
                    known = [i for i, x in enumerate(lefts) if x is left]
                    if not known:
                        lefts.append(left)
                    index = known[0] if known else len(lefts) - 1
                    unit_index[id(left), u] = len(units)
                    units.append((index, [k * rows + u * unit for k in range(shards)], unit))
                items.append((s, unit_index[id(left), u], len(rights) - 2, offset, width))
                offset += width
        widths.append(offset)
    out_specs = [pl.BlockSpec((2, shards * unit, w), lambda e, at: (e, 0, 0)) for w in widths]
    counts = (len(lefts), len(rights), len(arrived), len(widths), len(units))
    flops = sum(2 * rights[i[2]].shape[0] * shards * unit * i[4] for i in items) * pieces
    return pl.pallas_call(
        functools.partial(grads_kernel, units, items, counts),
        out_shape=[jax.ShapeDtypeStruct((pieces, shards * unit, w), BF16) for w in widths],
        grid_spec=pltpu.PrefetchScalarGridSpec(
            num_scalar_prefetch=1,
            grid=(pieces // 2,),
            in_specs=[pl.BlockSpec(x.shape, lambda e, at: (0, 0)) for x in lefts]
            + right_specs
            + out_specs[: len(arrived)],
            out_specs=out_specs,
            scratch_shapes=[
                pltpu.VMEM((shards * unit, lefts[u[0]].shape[0]), BF16) for u in units
            ],
        ),
        compiler_params=pltpu.CompilerParams(vmem_limit_bytes=VMEM_LIMIT),
        cost_estimate=pl.CostEstimate(
            flops=flops, bytes_accessed=8 * pieces * shards * unit * sum(widths), transcendentals=0
        ),
        name="grads",
    )(jnp.stack(at).astype(jnp.int32), *lefts, *rights, *arrived)


def fold_sent(streams):
    return [x[x.shape[0] // 2 :] for x in streams]


def fold(streams, arrived):
    return [
        (x[: x.shape[0] // 2].astype(F32) + a.astype(F32)).astype(BF16)
        for x, a in zip(streams, arrived)
    ]


def fold_swap(sent, step):
    bits = [plane_order(bool(s))[::-1][step] for s in range(len(sent))]
    return [dp_swap(x, bit) for x, bit in zip(sent, bits)]


def z_parts(streams, unit):
    shards = lax.axis_size("shard")
    z = lax.axis_index("shard")
    whole = jnp.concatenate([x[0] for x in streams], axis=1) if len(streams) > 1 else streams[0][0]

    def part(k):
        return lax.dynamic_slice_in_dim(whole, ((z + k) % shards) * unit, unit, axis=0)

    return part(0), [part(k) for k in range(1, shards)]


def z_sum(mine, arrived, streams):
    total = mine.astype(F32)
    for a in arrived:
        total = total + a.astype(F32)
    total = total.astype(BF16)
    parts, start = [], 0
    for x in streams:
        parts.append(total[None, :, start : start + x.shape[2]])
        start += x.shape[2]
    return parts


def widen_units_kernel(unit, parts, pieces, at_ref, *refs):
    step = pl.program_id(0)
    outs = refs[-len(parts) :]

    def move(far):
        for out_ref, (stream, offset, units, width) in zip(outs, parts):
            ref = refs[2 * stream + far]
            for u in range(units):
                out_ref[u * unit : (u + 1) * unit, :] = ref[
                    0, :, offset + u * width : offset + (u + 1) * width
                ].astype(F32)

    @pl.when(step < pieces)
    def _():
        move(0)

    @pl.when(step >= pieces)
    def _():
        move(1)


def widen_units(bundle, unit, weights):
    count_dp = lax.axis_size("dp")
    columns, specs, operands, parts, out_specs, shapes = [], [], [], [], [], []
    offsets = [0] * len(bundle)
    for s, (near, far) in enumerate(bundle):
        pieces = near.shape[0]
        columns += pieces_of(plane_order(bool(s)))[1]
        taken = (1,) + near.shape[1:]
        specs += [
            pl.BlockSpec(taken, lambda i, at: (jnp.minimum(i, pieces - 1), 0, 0)),
            pl.BlockSpec(taken, lambda i, at: (jnp.maximum(i - pieces, 0), 0, 0)),
        ]
        operands += [near, far]
    for w, s in weights:
        rows, total = w.shape
        width = total // count_dp
        parts.append((s, offsets[s], rows // unit, width))
        offsets[s] += rows // unit * width
        shapes.append(jax.ShapeDtypeStruct((rows, total), F32))
        out_specs.append(
            pl.BlockSpec((rows, width), lambda i, at, s=s: (0, at[s * count_dp + i]))
        )
    return pl.pallas_call(
        functools.partial(widen_units_kernel, unit, parts, pieces),
        out_shape=shapes,
        grid_spec=pltpu.PrefetchScalarGridSpec(
            num_scalar_prefetch=1, grid=(count_dp,), in_specs=specs, out_specs=out_specs
        ),
        compiler_params=pltpu.CompilerParams(vmem_limit_bytes=VMEM_LIMIT),
        name="widen",
    )(jnp.stack(columns).astype(jnp.int32), *operands)


def dot_nt(a, b):
    return lax.dot_general(a, b, (((1,), (1,)), ((), ())), preferred_element_type=F32)


def dot_tn(a, b):
    return lax.dot_general(a, b, (((0,), (0,)), ((), ())), preferred_element_type=F32)


def dot_nn(a, b):
    return lax.dot_general(a, b, (((1,), (0,)), ((), ())), preferred_element_type=F32)


def inverse_rms(v):
    return lax.rsqrt(jnp.mean(v * v, axis=-1, keepdims=True) + EPS)


def turn(u):
    return pltpu.roll(u, HEAD_WIDTH // 2, 1)


def norm_rope(v, gain, cosine, sine):
    u = v * inverse_rms(v) * gain
    return u * cosine + turn(u) * sine


def norm_rope_back(grad, v, gain, cosine, sine):
    r = inverse_rms(v)
    du = grad * cosine + turn(grad * sine)
    scaled = gain * du
    dv = r * scaled - v * (r * r * r) * jnp.mean(scaled * v, axis=-1, keepdims=True)
    return dv, du * v * r


def masked_exp(q, k, key_place, q_place, q_start):
    scores = dot_nt(q, k)
    allowed = (key_place <= q_place) & (key_place >= q_start)
    return jnp.where(allowed, jnp.exp2(scores * EXP2_SCALE), 0.0)


def load_queries(q_ref, gain_ref, cos_ref, sin_ref, held_ref, block):
    gain = gain_ref[...]
    for slot in range(2):
        rows = slice(slot * block, (slot + 1) * block)
        for head in range(2):
            v = q_ref[rows, head * HEAD_WIDTH : (head + 1) * HEAD_WIDTH]
            rotated = norm_rope(v, gain, cos_ref[rows, :], sin_ref[rows, :])
            held_ref[slot, head * block : (head + 1) * block, :] = rotated.astype(BF16)


def attend_kernel(
    sel_ref, q_ref, k_ref, v_ref, cos_ref, sin_ref, qg_ref, kg_ref, kp_ref, qp_ref, qs_ref,
    out_ref, held, acc, total,
):
    block = q_ref.shape[0] // 2
    pairs = k_ref.shape[0] // block
    load_queries(q_ref, qg_ref, cos_ref, sin_ref, held, block)
    for p in range(pairs):
        rows = slice(p * block, (p + 1) * block)
        slot = p if p < 2 else sel_ref[p - 2]
        k = norm_rope(k_ref[rows, :], kg_ref[...], cos_ref[rows, :], sin_ref[rows, :]).astype(BF16)
        e = masked_exp(held[slot], k, kp_ref[:, rows], qp_ref[slot], qs_ref[slot])
        added = dot_nn(e.astype(BF16), v_ref[rows, :])
        summed = jnp.sum(e, axis=-1, keepdims=True)
        if p < 2:
            acc[slot] = added
            total[slot] = summed
        else:
            acc[slot] += added
            total[slot] += summed
    for slot in range(2):
        value = (acc[slot] / total[slot]).astype(out_ref.dtype)
        for head in range(2):
            out_ref[
                slot * block : (slot + 1) * block, head * HEAD_WIDTH : (head + 1) * HEAD_WIDTH
            ] = value[head * block : (head + 1) * block, :]


def attend_back_kernel(
    sel_ref, q_ref, k_ref, v_ref, cos_ref, sin_ref, qg_ref, kg_ref, kp_ref, qp_ref, qs_ref,
    att_ref, gatt_ref, dq_ref, dk_ref, dv_ref, dqg_ref, dkg_ref,
    held, keys, grads, dots, total, raised, dq_acc,
):
    block = q_ref.shape[0] // 2
    pairs = k_ref.shape[0] // block
    load_queries(q_ref, qg_ref, cos_ref, sin_ref, held, block)
    for slot in range(2):
        rows = slice(slot * block, (slot + 1) * block)
        for head in range(2):
            columns = slice(head * HEAD_WIDTH, (head + 1) * HEAD_WIDTH)
            there = slice(head * block, (head + 1) * block)
            g = gatt_ref[rows, columns]
            grads[slot, there, :] = g
            dots[slot, there, :] = jnp.sum(
                g.astype(F32) * att_ref[rows, columns].astype(F32), axis=-1, keepdims=True
            )
    for p in range(pairs):
        rows = slice(p * block, (p + 1) * block)
        slot = p if p < 2 else sel_ref[p - 2]
        k = norm_rope(k_ref[rows, :], kg_ref[...], cos_ref[rows, :], sin_ref[rows, :]).astype(BF16)
        keys[rows, :] = k
        e = masked_exp(held[slot], k, kp_ref[:, rows], qp_ref[slot], qs_ref[slot])
        raised[p] = e
        summed = jnp.sum(e, axis=-1, keepdims=True)
        if p < 2:
            total[slot] = summed
        else:
            total[slot] += summed
    total[...] = 1.0 / total[...]

    @pl.when(pl.program_id(0) == 0)
    def _():
        dqg_ref[...] = jnp.zeros_like(dqg_ref)
        dkg_ref[...] = jnp.zeros_like(dkg_ref)

    for p in range(pairs):
        rows = slice(p * block, (p + 1) * block)
        slot = p if p < 2 else sel_ref[p - 2]
        g = grads[slot]
        shares = raised[p] * total[slot]
        dshares = dot_nt(g, v_ref[rows, :])
        dscores = (shares * (dshares - dots[slot])).astype(BF16)
        dv_ref[rows, :] = dot_tn(shares.astype(BF16), g).astype(dv_ref.dtype)
        added = dot_nn(dscores, keys[rows, :])
        if p < 2:
            dq_acc[slot] = added
        else:
            dq_acc[slot] += added
        dk = dot_tn(dscores, held[slot]) * SCALE
        dv, dgain = norm_rope_back(
            dk, k_ref[rows, :], kg_ref[...], cos_ref[rows, :], sin_ref[rows, :]
        )
        dk_ref[rows, :] = dv.astype(dk_ref.dtype)
        dkg_ref[...] += jnp.sum(dgain, axis=0, keepdims=True)
    for slot in range(2):
        rows = slice(slot * block, (slot + 1) * block)
        for head in range(2):
            columns = slice(head * HEAD_WIDTH, (head + 1) * HEAD_WIDTH)
            dv, dgain = norm_rope_back(
                dq_acc[slot, head * block : (head + 1) * block, :] * SCALE,
                q_ref[rows, columns],
                qg_ref[...],
                cos_ref[rows, :],
                sin_ref[rows, :],
            )
            dq_ref[rows, columns] = dv.astype(dq_ref.dtype)
            dqg_ref[...] += jnp.sum(dgain, axis=0, keepdims=True)


def attention_specs(count, total):
    pair = HEADS // KV_HEADS * HEAD_WIDTH
    fixed2 = lambda h, sel: (0, 0)
    fixed3 = lambda h, sel: (0, 0, 0)
    by_head = lambda h, sel: (0, h)
    q_spec = pl.BlockSpec((count, pair), by_head)
    k_spec = pl.BlockSpec((total, HEAD_WIDTH), by_head)
    inputs = [
        q_spec,
        k_spec,
        k_spec,
        pl.BlockSpec((total, HEAD_WIDTH), fixed2),
        pl.BlockSpec((total, HEAD_WIDTH), fixed2),
        pl.BlockSpec((1, HEAD_WIDTH), fixed2),
        pl.BlockSpec((1, HEAD_WIDTH), fixed2),
        pl.BlockSpec((1, total), fixed2),
        pl.BlockSpec((2, count, 1), fixed3),
        pl.BlockSpec((2, count, 1), fixed3),
    ]
    return q_spec, k_spec, pl.BlockSpec((1, HEAD_WIDTH), fixed2), inputs


def attention_cost(count, total, products):
    scores = HEADS * count // 2 * total
    return pl.CostEstimate(
        flops=products * 2 * HEAD_WIDTH * scores,
        bytes_accessed=16 * HEAD_WIDTH * HEADS * total,
        transcendentals=scores,
    )


def attend(sel, count, total, operands):
    q_spec, _, _, inputs = attention_specs(count, total)
    return pl.pallas_call(
        attend_kernel,
        out_shape=jax.ShapeDtypeStruct((count, HEADS * HEAD_WIDTH), BF16),
        grid_spec=pltpu.PrefetchScalarGridSpec(
            num_scalar_prefetch=1,
            grid=(KV_HEADS,),
            in_specs=inputs,
            out_specs=q_spec,
            scratch_shapes=[
                pltpu.VMEM((2, count, HEAD_WIDTH), BF16),
                pltpu.VMEM((2, count, HEAD_WIDTH), F32),
                pltpu.VMEM((2, count, 1), F32),
            ],
        ),
        compiler_params=pltpu.CompilerParams(vmem_limit_bytes=VMEM_LIMIT),
        cost_estimate=attention_cost(count, total, 2),
        name="attend",
    )(sel, *operands)


def attend_back(sel, count, total, operands):
    q_spec, k_spec, gain_spec, inputs = attention_specs(count, total)
    block = count // 2
    width = KV_HEADS * HEAD_WIDTH
    return pl.pallas_call(
        attend_back_kernel,
        out_shape=(
            jax.ShapeDtypeStruct((count, HEADS * HEAD_WIDTH), BF16),
            jax.ShapeDtypeStruct((total, width), BF16),
            jax.ShapeDtypeStruct((total, width), BF16),
            jax.ShapeDtypeStruct((1, HEAD_WIDTH), F32),
            jax.ShapeDtypeStruct((1, HEAD_WIDTH), F32),
        ),
        grid_spec=pltpu.PrefetchScalarGridSpec(
            num_scalar_prefetch=1,
            grid=(KV_HEADS,),
            in_specs=inputs + [q_spec, q_spec],
            out_specs=[q_spec, k_spec, k_spec, gain_spec, gain_spec],
            scratch_shapes=[
                pltpu.VMEM((2, count, HEAD_WIDTH), BF16),
                pltpu.VMEM((total, HEAD_WIDTH), BF16),
                pltpu.VMEM((2, count, HEAD_WIDTH), BF16),
                pltpu.VMEM((2, count, 1), F32),
                pltpu.VMEM((2, count, 1), F32),
                pltpu.VMEM((total // block, count, block), F32),
                pltpu.VMEM((2, count, HEAD_WIDTH), F32),
            ],
        ),
        compiler_params=pltpu.CompilerParams(vmem_limit_bytes=VMEM_LIMIT),
        cost_estimate=attention_cost(count, total, 5),
        name="attend_back",
    )(sel, *operands)


def rms_back(grad, v, gain):
    r = inverse_rms(v)
    scaled = grad * gain
    dv = r * scaled - v * (r * r * r) * jnp.mean(scaled * v, axis=-1, keepdims=True)
    return dv, jnp.sum(grad * v * r, axis=0)


def matmul(a, b):
    return jnp.dot(a, b, preferred_element_type=F32)


def body(
    tokens,
    attn_gain,
    w_query,
    w_key,
    w_value,
    q_gain,
    k_gain,
    w_out,
    mlp_gain,
    w_gate,
    w_up,
    w_down,
    segments,
    spans,
    out_grad,
):
    shards = lax.axis_size("shard")
    z = lax.axis_index("shard")
    count = tokens.shape[0]
    block = count // 2
    total = block * (shards + 1)
    span_row = spans[0]
    segment_row = segments[0]

    def span_of(index):
        return lax.dynamic_index_in_dim(span_row, index % shards, keepdims=False)

    span = span_of(z)
    slots = []
    remote_own = []
    sel = []
    numbers = [span, 2 * shards - 1 - span]
    for k in range(1, shards):
        slot = jnp.where(span < span_of(z + k), 0, 1)
        slots.append(slot)
        remote_own.append(lax.dynamic_slice_in_dim(tokens, slot * block, block, axis=0))
        other = span_of(z - k + shards)
        sel.append(jnp.where(other < span, 0, 1))
        numbers.append(jnp.where(other < span, other, 2 * shards - 1 - other))
    sel = jnp.stack(sel).astype(jnp.int32)

    sizes = [attn_gain.shape[0], mlp_gain.shape[0], q_gain.shape[0], k_gain.shape[0]]
    own_gains = jnp.concatenate([attn_gain, mlp_gain, q_gain, k_gain])
    unit = w_query.shape[0]
    count_dp = lax.axis_size("dp")
    bundled = all(
        w.shape[1] % (128 * count_dp) == 0 and w.shape[0] % unit == 0
        for w in (w_query, w_key, w_value, w_out, w_gate, w_up, w_down)
    ) and count_dp == 8
    if bundled:

        def own_pieces(streams):
            own = [
                jnp.concatenate([own_piece(w, unit, bool(s)) for w in stream], axis=1)
                for s, stream in enumerate(streams)
            ]
            return jnp.concatenate(own, axis=1), own[0].shape[1]

        def fetch(both):
            return [z_shift(both, k) for k in range(1, shards)]

        def streams_of(got, split):
            return [
                jnp.stack([g[:unit, :split] for g in got])[None],
                jnp.stack([g[:unit, split:] for g in got])[None],
            ]

        def widely(held):
            for step in range(1, len(plane_order(False))):
                held = join(held, grow(held, step - 1))
            return held, grow(held, len(plane_order(False)) - 1)

        def cores(held, arrived):
            return [[h, a, dp_swap(h, 0), dp_swap(a, 0)] for h, a in zip(held, arrived)]

        both, split_attn = own_pieces([[w_query], [w_key, w_value]])
        room = 16 * both.shape[1]
        packed = jnp.pad(own_gains, (0, room - own_gains.shape[0])).reshape(16, both.shape[1])
        first = fetch(jnp.concatenate([both, packed], axis=0))
        gains = jnp.stack(
            [own_gains] + [g[unit:].reshape(-1)[: own_gains.shape[0]] for g in first]
        )
        remote = [z_shift(x, k + 1) for k, x in enumerate(after(first, remote_own))]
        held, arrived = widely(streams_of(first, split_attn))
        held, arrived = after(remote, (held, arrived))
        near_q, near_kv = cores(held, arrived)
        both, split_out = own_pieces([[w_gate], [w_out]])
        second = fetch(after((near_q, near_kv), both))
        piece = w_key.shape[1] // count_dp
        full_query = place_units(w_query, near_q, unit, 0, False)
        full_key = place_units(w_key, near_kv, unit, 0, True)
        full_value = place_units(w_value, near_kv, unit, piece, True)
    else:
        gains = jnp.stack([own_gains] + [z_shift(own_gains, k) for k in range(1, shards)])
        remote = [z_shift(x, k + 1) for k, x in enumerate(remote_own)]
        full_query = gather_weight(w_query, False)
        full_key = gather_weight(w_key, True)
        full_value = gather_weight(w_value, True)
        full_out = gather_weight(w_out, True)
        full_gate = gather_weight(w_gate, False)
        full_up = gather_weight(w_up, True)
        full_down = gather_weight(w_down, False)

    order = (z - jnp.arange(shards)) % shards
    pick = order[:, None] == jnp.arange(shards)[None, :]
    gains = jnp.sum(jnp.where(pick[:, :, None], gains.astype(F32)[None], 0.0), axis=1)
    parts = []
    start = 0
    for size in sizes:
        parts.append(gains[:, start : start + size].reshape(1, shards * size))
        start += size
    attn_g, mlp_g, q_g, k_g = parts

    place = jnp.concatenate([n * block + jnp.arange(block, dtype=jnp.int32) for n in numbers])
    seg = jnp.concatenate([lax.dynamic_slice_in_dim(segment_row, n * block, block) for n in numbers])
    doc_start = jnp.sum((segment_row[None, :] < seg[:, None]).astype(jnp.int32), axis=1)
    steps = jnp.arange(HEAD_WIDTH // 2, dtype=F32) * (2.0 / HEAD_WIDTH)
    inverse = jnp.power(F32(THETA), -steps)
    angles = (place - doc_start).astype(F32)[:, None] * inverse[None, :]
    cosine, sine = jnp.cos(angles), jnp.sin(angles)
    cosine = jnp.concatenate([cosine, cosine], axis=1)
    sine = jnp.concatenate([-sine, sine], axis=1)

    def by_slot(v):
        v = v[:count].reshape(2, 1, block, 1)
        return jnp.concatenate([v, v], axis=1).reshape(2, count, 1)

    rows = jnp.concatenate([tokens] + remote, axis=0).astype(F32)
    normed = (rows * inverse_rms(rows) * attn_g).astype(BF16)
    queries = matmul(normed[:count], full_query)
    keys_pre = matmul(normed, full_key)
    values = matmul(normed, full_value).astype(BF16)
    operands = (
        queries, keys_pre, values, cosine, sine, q_g, k_g,
        place[None, :], by_slot(place), by_slot(doc_start),
    )
    if bundled:
        second, operands = lax.optimization_barrier((second, operands))
        both, split_down = own_pieces([[w_up], [w_down]])
        third = fetch(after(second, both))
        held = streams_of(second, split_out)
        held = join(held, grow(held, 0)) if len(plane_order(False)) > 1 else held
    attended = attend(sel, count, total, operands)
    if bundled:
        held, third, attended = lax.optimization_barrier((held, third, attended))
        later = streams_of(third, split_down)
        later_arrived = grow(later, 0)
        arrived = grow(held, 1)
        later, later_arrived, held, arrived = lax.optimization_barrier(
            (later, later_arrived, held, arrived)
        )
        near_gate, near_out = cores(held, arrived)
        later = join(later, later_arrived)
        later, near_gate, near_out = lax.optimization_barrier((later, near_gate, near_out))
        later_arrived = grow(later, 1)
        full_out = place_units(w_out, near_out, unit, 0, True)
        full_gate = place_units(w_gate, near_gate, unit, 0, False)
    residual = tokens.astype(F32) + matmul(attended, full_out)
    mixed = (residual * inverse_rms(residual) * mlp_g).astype(BF16)
    gate = matmul(mixed, full_gate)
    if bundled:
        later_arrived, gate = lax.optimization_barrier((later_arrived, gate))
        near_up, near_down = cores(later, later_arrived)
        full_up = place_units(w_up, near_up, unit, 0, False)
        full_down = place_units(w_down, near_down, unit, 0, True)
    upward = matmul(mixed, full_up)
    sig = jax.nn.sigmoid(gate)
    hidden = (gate * sig * upward).astype(BF16)
    result = (residual + matmul(hidden, full_down)).astype(BF16)

    def swap_cores(streams):
        return [dp_swap(x, 0) for x in streams]

    def z_send(streams, chained=False):
        mine, sent = z_parts(streams, unit)
        got = []
        for k, x in enumerate(sent):
            got.append(z_shift(after(got[-1], x) if chained and got else x, k + 1))
        return mine, got

    barrier = lax.optimization_barrier

    grad_rows = out_grad
    if bundled:
        down_pairs = [[(hidden, out_grad)]]
        theirs = grads(down_pairs, unit, False)
        theirs, grad_rows = barrier((theirs, out_grad))
        down_core = swap_cores(theirs)
    else:
        grad_w_down = reduce_weight(hidden, out_grad, False)
    grad_hidden = dot_nt(grad_rows, full_down)
    grad_gate = (grad_hidden * upward * sig * (1.0 + gate * (1.0 - sig))).astype(BF16)
    grad_upward = (grad_hidden * gate * sig).astype(BF16)
    if bundled:
        down_core, grad_gate, grad_upward = barrier((down_core, grad_gate, grad_upward))
        down_sum = grads(down_pairs, unit, True, down_core)
        down_sum, grad_gate, grad_upward = barrier((down_sum, grad_gate, grad_upward))
        down_first = fold_swap(fold_sent(down_sum), 0)
    grad_mixed = dot_nt(grad_gate, full_gate) + dot_nt(grad_upward, full_up)
    grad_residual, grad_mlp_gain = rms_back(grad_mixed, residual, mlp_g)
    grad_residual = grad_residual + out_grad.astype(F32)
    grad_branch = grad_residual.astype(BF16)
    if bundled:
        mlp_pairs = [[(mixed, grad_gate)], [(mixed, grad_upward), (attended, grad_branch)]]
        theirs = grads(mlp_pairs, unit, False)
        theirs, branch = barrier((theirs, grad_branch))
        mlp_core = swap_cores(theirs)
        grad_attended = dot_nt(branch, full_out).astype(BF16)
        mlp_core, grad_attended = barrier((mlp_core, grad_attended))
        mlp_sum = grads(mlp_pairs, unit, True, mlp_core)
        mlp_sum, down_first, grad_attended = barrier((mlp_sum, down_first, grad_attended))
        down_sum = fold(down_sum, down_first)
        down_second = fold_swap(fold_sent(down_sum), 1)
        mlp_first = fold_swap(fold_sent(mlp_sum), 0)
    else:
        grad_attended = dot_nt(grad_branch, full_out).astype(BF16)
        grad_w_gate = reduce_weight(mixed, grad_gate, False)
        grad_w_up = reduce_weight(mixed, grad_upward, True)
        grad_w_out = reduce_weight(attended, grad_branch, True)

    dq, dk, dv, grad_q_gain, grad_k_gain = attend_back(
        sel, count, total, operands + (attended, grad_attended)
    )
    if bundled:
        mlp_first, down_second, dq, dk, dv = barrier((mlp_first, down_second, dq, dk, dv))
        down_sum = fold(down_sum, down_second)
        down_mine, down_z = z_send(down_sum, True)
        mlp_sum = fold(mlp_sum, mlp_first)
        mlp_second = fold_swap(fold_sent(mlp_sum), 1)
        attn_pairs = [[(normed, dq)], [(normed, dk), (normed, dv)]]
        theirs = grads(attn_pairs, unit, False)
    grad_normed_kv = dot_nt(dk, full_key) + dot_nt(dv, full_value)
    terms = [
        grad_normed_kv[count + (k - 1) * block : count + k * block].astype(BF16)
        for k in range(1, shards)
    ]
    if bundled:
        mlp_second, theirs = barrier((mlp_second, theirs))
        attn_core = swap_cores(theirs)
        mlp_sum = fold(mlp_sum, mlp_second)
    back = []
    for k, term in enumerate(terms):
        back.append(z_shift(after(back[-1], term) if back else term, shards - k - 1))
    grad_normed_own = grad_normed_kv[:count] + dot_nt(dq, full_query)
    partial = jnp.concatenate([grad_normed_own, grad_normed_kv[count:]], axis=0)
    grad_attn_gain = jnp.sum(partial * rows * inverse_rms(rows), axis=0)
    gain_sum = jnp.concatenate(
        [grad_attn_gain, grad_mlp_gain, grad_q_gain[0], grad_k_gain[0]]
    ).reshape(-1, HEAD_WIDTH)
    if bundled:
        mlp_mine, mlp_z = z_send(mlp_sum, True)
        attn_core, grad_normed_own = barrier((attn_core, grad_normed_own))
        attn_sum = grads(attn_pairs, unit, True, attn_core)
        attn_first = fold_swap(fold_sent(attn_sum), 0)
        gain_other = dp_swap(gain_sum, 0)
        attn_first, back, gain_other, down_z = barrier((attn_first, back, gain_other, down_z))
        down_sum = z_sum(down_mine, down_z, down_sum)
        gain_sum = gain_sum + gain_other
        attn_sum = fold(attn_sum, attn_first)
        attn_second = fold_swap(fold_sent(attn_sum), 1)
        gain_other = dp_swap(gain_sum, 1)
        attn_second, mlp_z, gain_other = barrier((attn_second, mlp_z, gain_other))
        gain_sum = gain_sum + gain_other
        attn_sum = fold(attn_sum, attn_second)
        attn_mine, attn_z = z_send(attn_sum)
        gain_sum = gain_sum + dp_swap(gain_sum, 2)
        mlp_sum = z_sum(mlp_mine, mlp_z, mlp_sum)

        def whole(streams):
            for step in range(len(plane_order(False))):
                streams = join(streams, grow(streams, step))
            return [(x, dp_swap(x, 0)) for x in streams]

        mlp_sum = [jnp.concatenate([down_sum[0], mlp_sum[0]], axis=2), mlp_sum[1]]
        mlp_whole, attn_z = barrier((whole(mlp_sum), attn_z))
        grad_w_down, grad_w_gate, grad_w_up, grad_w_out = widen_units(
            mlp_whole, unit, [(w_down, 0), (w_gate, 0), (w_up, 1), (w_out, 1)]
        )
        gain_sum = sum([z_shift(gain_sum, k) for k in range(1, shards)], gain_sum)
        attn_sum = z_sum(attn_mine, attn_z, attn_sum)
        grad_w_query, grad_w_key, grad_w_value = widen_units(
            whole(attn_sum), unit, [(w_query, 0), (w_key, 1), (w_value, 1)]
        )
    else:
        for bit in range(count_dp.bit_length() - 1):
            gain_sum = gain_sum + dp_swap(gain_sum, bit)
        gain_sum = sum([z_shift(gain_sum, k) for k in range(1, shards)], gain_sum)
        grad_w_query = reduce_weight(normed[:count], dq, False)
        grad_w_key = reduce_weight(normed, dk, True)
        grad_w_value = reduce_weight(normed, dv, True)

    for slot, term in zip(slots, back):
        term = term.astype(F32)
        first = jnp.where(slot == 0, term, 0.0)
        grad_normed_own = grad_normed_own + jnp.concatenate([first, term - first], axis=0)
    grad_tokens = grad_residual + rms_back(grad_normed_own, tokens.astype(F32), attn_g)[0]

    packed = gain_sum.reshape(-1)
    gain_grads = []
    start = 0
    for size in sizes:
        gain_grads.append(lax.dynamic_slice_in_dim(packed, start + z * size, size))
        start += size * shards

    return (
        result,
        grad_tokens,
        gain_grads[0],
        grad_w_query,
        grad_w_key,
        grad_w_value,
        gain_grads[2],
        gain_grads[3],
        grad_w_out,
        gain_grads[1],
        grad_w_gate,
        grad_w_up,
        grad_w_down,
    )


def solution(mesh):
    rows = P("shard", None)
    both = P(("dp", "shard"), None)
    placed = (
        both, P("shard"), rows, rows, rows, P("shard"), P("shard"), rows, P("shard"), rows, rows, rows,
        P("dp", None), P("dp", None), both,
    )
    return jax.shard_map(
        body,
        mesh=mesh,
        in_specs=placed,
        out_specs=(
            both, both, P("shard"), rows, rows, rows, P("shard"), P("shard"), rows, P("shard"),
            rows, rows, rows,
        ),
        check_vma=False,
    )
```
